512 devices in a mesh: feed: 32 (over z_hi, y), tm: 16 (over x, z_lo, core).
Axes of the slice: x: 4, y: 8, z: 8 (z_hi: 4, z_lo: 2; z = z_hi * 2 + z_lo), core: 2. Of those that a mesh axis runs over, the one named last changes fastest.
Arguments:
- voltages: bfloat16 [2048, 262144], P('feed', 'tm'), may hold values from -6 to 6
- pfb_coeffs: float32 [4, 2048], replicated, may hold values from 0.25 to 1.75
- flags: int32 [128, 64], P('tm'), may hold values from 0 to 1, as said below
- channel_order: int32 [64], replicated, may hold values from 0 to 63, each once
Outputs:
- vis_real: bfloat16 [64, 2048, 2048], P('feed', 'tm')
- vis_imag: bfloat16 [64, 2048, 2048], P('feed', 'tm')
The draws below stay inside these ranges and needn't reach their ends.
Inputs may be any that keep to these rules, and one draw needn't show every extreme that they name: `flags`: some window channels are flagged in every spectrum.
All inputs are finite; a program needn't handle non-finite values.
Results may differ from the reference program's by a relative error of at most 0.0059.
Values may be sent and summed in bfloat16 or wider, within the bound.
A program may use at most 64 MiB of HBM per device.

```python
import jax
import jax.numpy as jnp
from jax import lax

NIN = 2048
TAPS = 4
WIN = 64
CHAN0 = 448
NFFT = 2048
SPECTRA = 128


def draw_flags(key, part):
    key = jax.random.fold_in(key, 7)
    key_chan, key_spec, key_pick = jax.random.split(key, 3)
    dead = jax.random.randint(key_chan, (WIN,), 0, 8) == 0
    pick = jax.random.randint(key_pick, (), 0, WIN)
    dead = dead | (jnp.arange(WIN) == pick)
    keep = jax.random.randint(key_spec, (SPECTRA, WIN), 0, 8) != 0
    return jnp.where(keep & jnp.logical_not(dead)[None, :], 1, 0).astype(jnp.int32)


def steps_of(key, extent, cuts, low, largest):
    def one(position, shards_of):
        draws = jax.random.uniform(jax.random.fold_in(jax.random.fold_in(key, 6), position), (shards_of,), jnp.float32, low / len(cuts), largest / len(cuts))
        return jnp.repeat(jnp.exp(draws), extent[position] // shards_of).reshape((-1,) + (1,) * (len(extent) - position - 1))

    factor_of = one(*cuts[0])
    for cut in cuts[1:]:
        factor_of = factor_of * one(*cut)
    return factor_of


def scatter_about(own_key, dims, deviation, bound, cuts=(), kind=jnp.bfloat16):
    factor_of = steps_of(own_key, dims, cuts, -0.22, 0.18) if cuts else 1.0
    entries = jax.random.normal(own_key, dims, jnp.float32) * deviation * factor_of
    return jnp.minimum(jnp.maximum(entries, -bound), bound).astype(kind)


def setup_inputs(seed: int = 0) -> dict:
    key_of = jax.random.split(jax.random.key(seed), 5)
    return {
        "voltages": scatter_about(key_of[0], (NIN, SPECTRA * NFFT), 1.0, 6.0, ((0, 32), (1, 16))),
        "pfb_coeffs": jnp.clip(jax.random.uniform(key_of[1], (TAPS, NFFT), jnp.float32, 0.25, 1.75), 0.25, 1.75),
        "flags": draw_flags(jax.random.fold_in(key_of[4], 71), 0),
        "channel_order": jax.random.permutation(key_of[3], WIN).astype(jnp.int32),
    }


def make_table(coeffs, order, chan_first):
    tap_count, frame_len = coeffs.shape
    window = order.shape[0]
    sample = jnp.arange(frame_len, dtype=jnp.int32)
    freq = chan_first + order.astype(jnp.int32)
    phase = (freq[None, :] * sample[:, None]) % frame_len
    angle = phase.astype(jnp.float32) * (2.0 * jnp.pi / frame_len)
    trig = jnp.stack([jnp.cos(angle), -jnp.sin(angle)], axis=2).reshape(frame_len, 2 * window)
    scale = (tap_count * frame_len / 2.0) ** -0.5
    table = coeffs[:, :, None] * trig[None, :, :] * scale
    return table.reshape(tap_count * frame_len, 2 * window).astype(jnp.bfloat16)


def reference(voltages, pfb_coeffs, flags, channel_order):
    table = make_table(pfb_coeffs, channel_order, CHAN0)
    block_inputs = min(64, NIN)
    padded = jnp.concatenate([jnp.zeros((NIN, (TAPS - 1) * NFFT), jnp.bfloat16), voltages], axis=1)
    blocks = padded.reshape(NIN // block_inputs, block_inputs, SPECTRA + TAPS - 1, NFFT)
    table_wide = table.astype(jnp.float32)

    def channelize(block):
        frames = jnp.concatenate([block[:, t:t + SPECTRA, :] for t in range(TAPS)], axis=2)
        return jnp.einsum("isk,kc->csi", frames.astype(jnp.float32), table_wide)

    raw = lax.map(channelize, blocks)
    raw = raw.transpose(1, 2, 0, 3).reshape(2 * WIN, SPECTRA, NIN)
    good = flags[:, channel_order].astype(jnp.float32)
    mask = jnp.repeat(good.T, 2, axis=0)
    spectra = (raw * mask[:, :, None]).astype(jnp.bfloat16)
    counts = jnp.sum(good, axis=0)
    denom = jnp.maximum(counts, 1.0)
    pairs = spectra.reshape(WIN, 2, SPECTRA, NIN)

    def correlate(item):
        pair, scale = item
        real_part, imag_part = pair[0], pair[1]
        full = jnp.concatenate([real_part, imag_part], axis=0)
        swapped = jnp.concatenate([imag_part, -real_part], axis=0)
        vis_re = jnp.dot(full.T, full, preferred_element_type=jnp.float32) / scale
        vis_im = jnp.dot(swapped.T, full, preferred_element_type=jnp.float32) / scale
        return vis_re.astype(jnp.bfloat16), vis_im.astype(jnp.bfloat16)

    vis_real, vis_imag = lax.map(correlate, (pairs, denom))
    return vis_real, vis_imag
```

```python
import functools
import math

import jax
import jax.numpy as jnp
from jax import lax
from jax.experimental import pallas as pl
from jax.experimental.pallas import tpu as pltpu
from jax.sharding import PartitionSpec as P

CHAN0 = 448
NF = 32
NT = 16
INPUTS = 64
FRAMES = 8
TAPS = 4
FRAME = 2048
COLS = 2048
HALF = COLS // 2
NCHAN = 4 * NF
MESH = pl.DeviceIdType.MESH
SINE = [(math.pi / 2) ** n / math.factorial(n) * (-1) ** (n // 2) for n in (1, 3, 5, 7, 9, 11)]

GATHER = {
    0: ("own", "all", "sib"),
    1: ("own", "all", "zed"),
    2: ("own", "all", "right"),
    3: ("own", "all", "left"),
    4: ("z", "all", "sib"),
    5: ("z", "all", "right"),
    6: ("z", "all", "left"),
    7: ("l", "all", "sib"),
    8: ("l", "lo", "right"),
    9: ("r", "all", "sib"),
    10: ("r", "hi", "left"),
    11: ("lz", "all", "sib"),
    12: ("lz", "lo", "right"),
    13: ("rz", "all", "sib"),
    14: ("rz", "hi", "left"),
    15: ("o", "lo", "sib"),
    16: ("o", "hi", "sib"),
    17: ("oz", "lo", "sib"),
    18: ("oz", "hi", "sib"),
}
EVENTS = len(GATHER)


def kernel(volt, coef, flags, order, out_re, out_im, frames, table, prod, halo_out, halo_in, rows,
           send_buf, recv_buf, count_buf, full, stage_re, stage_im,
           load_sem, halo_sem, turn_sem, count_sem, gather_send, gather_recv, own_sem, store_sem):
    f32 = jnp.float32
    bf16 = jnp.bfloat16
    feed = lax.axis_index("feed")
    tm = lax.axis_index("tm")

    barrier = pltpu.get_barrier_semaphore()

    def greet(axis, here, count):
        def one(step, carry):
            peer = lax.rem(here + step, count)
            pl.semaphore_signal(barrier, inc=1, device_id={axis: peer}, device_id_type=MESH)
            return carry

        lax.fori_loop(1, count, one, 0)

    loads = []
    for f in (7, 6, 5, 4, 3, 2, 1, 0):
        load = pltpu.make_async_copy(
            volt.at[:, pl.ds(f * FRAME, FRAME)], frames.at[pl.ds(f * INPUTS, INPUTS), :], load_sem.at[f]
        )
        load.start()
        loads.append(load)
    greet("tm", tm, NT)
    greet("feed", feed, NF)

    c_row = lax.broadcasted_iota(jnp.int32, (NCHAN, 2 * NF), 0)
    k_col = lax.broadcasted_iota(jnp.int32, (NCHAN, 2 * NF), 1)
    pick = k_col == 2 * (c_row & (NF - 1)) + (c_row >> 6)
    order_f = order[...].astype(f32)
    place = jnp.sum(jnp.where(pick, order_f, 0.0), axis=1, keepdims=True)
    chan_of = place.astype(jnp.int32)
    freq = jnp.broadcast_to(chan_of + CHAN0, (NCHAN, 128))
    lane = lax.broadcasted_iota(jnp.int32, (NCHAN, 128), 1)
    part = (lax.broadcasted_iota(jnp.int32, (NCHAN, 128), 0) >> 5) & 1
    phase0 = freq * lane + part * (FRAME // 4)
    phase_step = freq * 128
    scale = (TAPS * FRAME / 2.0) ** (-0.5)

    def table_block(a, phase):
        cols = pl.ds(pl.multiple_of(a * 128, 128), 128)
        dist = jnp.abs((phase & (FRAME - 1)) - FRAME // 2).astype(f32)
        z = dist * (4.0 / FRAME) - 1.0
        z2 = z * z
        trig = jnp.full_like(z, SINE[-1])
        for term in SINE[-2::-1]:
            trig = trig * z2 + term
        trig = trig * z
        for t in range(TAPS):
            table[pl.ds(t * NCHAN, NCHAN), cols] = (trig * (coef[pl.ds(t, 1), cols] * scale)).astype(bf16)
        return phase + phase_step

    lax.fori_loop(0, FRAME // 128, table_block, phase0)

    hot = (lax.broadcasted_iota(jnp.int32, (NCHAN, 2 * NF), 1) == chan_of).astype(bf16)
    nt = (((1,), (1,)), ((), ()))
    good = lax.dot_general(flags[...].astype(f32).astype(bf16), hot, nt, preferred_element_type=f32)
    local = jnp.sum(good, axis=0, keepdims=True)
    lane1 = lax.broadcasted_iota(jnp.int32, (1, NCHAN), 1)
    counts = [
        jnp.sum(jnp.where(lane1 == feed + kl * 2 * NF, local, 0.0), axis=1, keepdims=True) for kl in range(2)
    ]
    sub8 = lax.broadcasted_iota(jnp.int32, (8, 128), 0)
    count_buf[tm] = jnp.where(sub8 < 4, counts[0], counts[1])

    for load in loads[:4]:
        load.wait()
    prod[pl.ds(256, 256), :] = lax.dot_general(
        frames[pl.ds(256, 256), :], table[...], nt, preferred_element_type=f32
    )

    def term(f, t):
        return prod[pl.ds(f * INPUTS, INPUTS), pl.ds(t * NCHAN, NCHAN)]

    def partial(s):
        terms = [term(s - 3 + t, t) for t in range(TAPS) if 0 <= s - 3 + t < FRAMES]
        total = terms[0]
        for other in terms[1:]:
            total = total + other
        return total

    for s in range(3):
        halo_out[pl.ds(s * INPUTS, INPUTS), :] = partial(FRAMES + s)

    pl.semaphore_wait(barrier, NT - 1 + NF - 1)

    halo = pltpu.make_async_remote_copy(
        src_ref=halo_out, dst_ref=halo_in, send_sem=halo_sem.at[0], recv_sem=halo_sem.at[1],
        device_id={"tm": lax.rem(tm + 1, NT)}, device_id_type=MESH,
    )
    halo.start()

    def send_count(step, carry):
        pltpu.make_async_remote_copy(
            src_ref=count_buf.at[tm], dst_ref=count_buf.at[tm],
            send_sem=count_sem.at[0], recv_sem=count_sem.at[1],
            device_id={"tm": lax.rem(tm + step, NT)}, device_id_type=MESH,
        ).start()
        return carry

    lax.fori_loop(1, NT, send_count, 0)

    for load in loads[4:]:
        load.wait()
    prod[pl.ds(0, 256), :] = lax.dot_general(
        frames[pl.ds(0, 256), :], table[...], nt, preferred_element_type=f32
    )

    def turn(j):
        pair = []
        for s in (2 * j, 2 * j + 1):
            value = partial(s)
            if s < 3:
                value = value + jnp.where(tm > 0, halo_in[pl.ds(s * INPUTS, INPUTS), :], 0.0)
            pair.append(value * good[s : s + 1, :])
        turned = jnp.concatenate(pair, axis=0).T
        for q in range(4):
            rows[:, q * 4 + j, :] = turned[q * NF : (q + 1) * NF, :]

    turn(3)
    turn(2)
    halo.wait_recv()
    turn(1)
    turn(0)
    send_buf[...] = rows[...].astype(bf16)

    def send_rows(step, carry):
        peer = lax.rem(feed + step, NF)
        pltpu.make_async_remote_copy(
            src_ref=send_buf.at[peer], dst_ref=recv_buf.at[feed],
            send_sem=turn_sem.at[0], recv_sem=turn_sem.at[1],
            device_id={"feed": peer}, device_id_type=MESH,
        ).start()
        return carry

    lax.fori_loop(1, NF, send_rows, 0)
    own = pltpu.make_async_copy(send_buf.at[feed], recv_buf.at[feed], own_sem)
    own.start()
    own.wait()
    others = recv_buf.at[pl.ds(0, NF - 1)]
    pltpu.make_async_copy(others, others, turn_sem.at[1]).wait()

    low = lax.broadcasted_iota(jnp.int32, (16, 128), 1) < INPUTS
    for g in range(NF // 2):
        one = recv_buf[2 * g].astype(f32)
        two = recv_buf[2 * g + 1].astype(f32)
        first = jnp.where(low, one, pltpu.roll(two, INPUTS, 1))
        second = jnp.where(low, pltpu.roll(one, INPUTS, 1), two)
        for kl in range(2):
            full[kl, tm, :, pl.ds(g * 128, 128)] = jnp.concatenate(
                [first[kl * 8 : kl * 8 + 8], second[kl * 8 : kl * 8 + 8]], axis=0
            ).astype(bf16)

    x, zed, core = tm // 4, lax.rem(tm // 2, 2), lax.rem(tm, 2)

    def at(dx, dz, dc):
        return lax.rem(x + dx, 4) * 4 + lax.rem(zed + dz, 2) * 2 + lax.rem(core + dc, 2)

    targets = {"sib": at(0, 0, 1), "zed": at(0, 1, 0), "right": at(1, 0, 0), "left": at(3, 0, 0)}
    blocks = {"own": (0, 0), "z": (0, 1), "l": (3, 0), "r": (1, 0), "lz": (3, 1), "rz": (1, 1), "o": (2, 0), "oz": (2, 1)}
    moves = {"sib": (0, 0, 1), "zed": (0, 1, 0), "right": (3, 0, 0), "left": (1, 0, 0)}
    lanes = {"all": pl.ds(0, COLS), "lo": pl.ds(0, HALF), "hi": pl.ds(HALF, HALF)}

    def view(kl, index, which):
        return full.at[kl, index, :, lanes[which]]

    def send(kl, event):
        block, which, target = GATHER[event]
        ref = view(kl, at(*blocks[block], 0), which)
        copy = pltpu.make_async_remote_copy(
            src_ref=ref, dst_ref=ref,
            send_sem=gather_send.at[kl, event], recv_sem=gather_recv.at[kl, event],
            device_id={"tm": targets[target]}, device_id_type=MESH,
        )
        copy.start()

    def arrived(kl, event):
        block, which, target = GATHER[event]
        dx, dz = blocks[block]
        mx, mz, mc = moves[target]
        ref = view(kl, at((dx + mx) % 4, (dz + mz) % 2, mc), which)
        pltpu.make_async_copy(ref, ref, gather_recv.at[kl, event]).wait()

    def sent(kl, event):
        block, which, _ = GATHER[event]
        ref = view(kl, at(*blocks[block], 0), which)
        pltpu.make_async_copy(ref, ref, gather_send.at[kl, event]).wait()

    def relay(kl, event, *following):
        arrived(kl, event)
        for after in following:
            send(kl, after)

    for kl in range(2):
        for event in (2, 3, 1, 0):
            send(kl, event)
    for kl in range(2):
        relay(kl, 1, 5, 6, 4)
        relay(kl, 2, 8, 7)
        relay(kl, 3, 10, 9)
    for kl in range(2):
        relay(kl, 5, 12, 11)
        relay(kl, 6, 14, 13)

    every = count_buf.at[pl.ds(0, NT - 1)]
    pltpu.make_async_copy(every, every, count_sem.at[1]).wait()
    total = jnp.sum(count_buf[...], axis=0)
    inverse = 1.0 / jnp.maximum(total, 1.0)

    mine = pl.ds(pl.multiple_of(tm * 128, 128), 128)
    stores = []

    def correlate(kl):
        left = full[kl, :, :, mine].reshape(32, 8, 128).astype(f32)
        swapped = jnp.concatenate([left[:, 4:], -left[:, :4]], axis=1)
        both = jnp.concatenate([left.reshape(256, 128).T, swapped.reshape(256, 128).T], axis=0).astype(bf16)
        factor = inverse[4 * kl : 4 * kl + 1, 0:1]

        def column(n, carry):
            cols = pl.ds(pl.multiple_of(n * 512, 512), 512)
            right = full[kl, :, :, cols].reshape(256, 512)
            result = jnp.dot(both, right, preferred_element_type=f32) * factor
            stage_re[kl, :, cols] = result[:128].astype(bf16)
            stage_im[kl, :, cols] = result[128:].astype(bf16)
            return carry

        lax.fori_loop(0, COLS // 512, column, 0)
        for n, (stage, out) in enumerate(((stage_re, out_re), (stage_im, out_im))):
            store = pltpu.make_async_copy(stage.at[kl], out.at[kl], store_sem.at[kl, n])
            store.start()
            stores.append(store)

    for kl in range(2):
        relay(kl, 8, 15)
        relay(kl, 10, 16)
        relay(kl, 12, 17)
        relay(kl, 14, 18)
        for event in (0, 4, 7, 9, 11, 13, 15, 16, 17, 18):
            arrived(kl, event)
        correlate(kl)

    halo.wait_send()
    pltpu.make_async_copy(every, every, count_sem.at[0]).wait()
    gone = send_buf.at[pl.ds(0, NF - 1)]
    pltpu.make_async_copy(gone, gone, turn_sem.at[0]).wait()
    for kl in range(2):
        for event in range(EVENTS):
            sent(kl, event)
    for store in stores:
        store.wait()


def body(voltages, pfb_coeffs, flags, channel_order):
    vmem = pl.BlockSpec(memory_space=pltpu.VMEM)
    anywhere = pl.BlockSpec(memory_space=pl.ANY)
    out = jax.ShapeDtypeStruct((2, 128, COLS), jnp.bfloat16)
    dma = pltpu.SemaphoreType.DMA
    return pl.pallas_call(
        kernel,
        out_shape=(out, out),
        in_specs=[anywhere, vmem, vmem, vmem],
        out_specs=(anywhere, anywhere),
        scratch_shapes=[
            pltpu.VMEM((FRAMES * INPUTS, FRAME), jnp.bfloat16),
            pltpu.VMEM((TAPS * NCHAN, FRAME), jnp.bfloat16),
            pltpu.VMEM((FRAMES * INPUTS, TAPS * NCHAN), jnp.float32),
            pltpu.VMEM((3 * INPUTS, NCHAN), jnp.float32),
            pltpu.VMEM((3 * INPUTS, NCHAN), jnp.float32),
            pltpu.VMEM((NF, 16, 128), jnp.float32),
            pltpu.VMEM((NF, 16, 128), jnp.bfloat16),
            pltpu.VMEM((NF, 16, 128), jnp.bfloat16),
            pltpu.VMEM((NT, 8, 128), jnp.float32),
            pltpu.VMEM((2, NT, 16, COLS), jnp.bfloat16),
            pltpu.VMEM((2, 128, COLS), jnp.bfloat16),
            pltpu.VMEM((2, 128, COLS), jnp.bfloat16),
            dma((FRAMES,)),
            dma((2,)),
            dma((2,)),
            dma((2,)),
            dma((2, EVENTS)),
            dma((2, EVENTS)),
            dma,
            dma((2, 2)),
        ],
        compiler_params=pltpu.CompilerParams(
            collective_id=0, has_side_effects=True, vmem_limit_bytes=32 * 1024 * 1024
        ),
        name="channelize_correlate",
    )(voltages, pfb_coeffs, flags, channel_order.reshape(1, -1))


def solution(mesh):
    return jax.shard_map(
        body,
        mesh=mesh,
        in_specs=(P("feed", "tm"), P(), P("tm", None), P()),
        out_specs=(P("feed", "tm", None), P("feed", "tm", None)),
        check_vma=False,
    )
```

```python
import functools
import math

import jax
import jax.numpy as jnp
from jax import lax
from jax.experimental import pallas as pl
from jax.experimental.pallas import tpu as pltpu
from jax.sharding import PartitionSpec as P

CHAN0 = 448
NF = 32
NT = 16
INPUTS = 64
FRAMES = 8
TAPS = 4
FRAME = 2048
COLS = 2048
HALF = COLS // 2
WIDE = 512
NCHAN = 4 * NF
MESH = pl.DeviceIdType.MESH
SINE = [(math.pi / 2) ** n / math.factorial(n) * (-1) ** (n // 2) for n in (1, 3, 5, 7, 9, 11)]

GATHER = {
    0: ("own", "all", "sib"),
    1: ("own", "all", "zed"),
    2: ("own", "all", "right"),
    3: ("own", "all", "left"),
    4: ("z", "all", "sib"),
    5: ("z", "all", "right"),
    6: ("z", "all", "left"),
    7: ("l", "all", "sib"),
    8: ("l", "lo", "right"),
    9: ("r", "all", "sib"),
    10: ("r", "hi", "left"),
    11: ("lz", "all", "sib"),
    12: ("lz", "lo", "right"),
    13: ("rz", "all", "sib"),
    14: ("rz", "hi", "left"),
    15: ("o", "lo", "sib"),
    16: ("o", "hi", "sib"),
    17: ("oz", "lo", "sib"),
    18: ("oz", "hi", "sib"),
}
EVENTS = len(GATHER)

FAR = sorted(
    ((dz, dy) for dz in range(4) for dy in range(8) if dz or dy),
    key=lambda step: -(2 * min(step[0], 4 - step[0]) + min(step[1], 8 - step[1])),
)


def kernel(volt, coef_hbm, flags_hbm, order_hbm, full, count_buf, coef, flags, order, frames, table, prod,
           rows, send_buf, recv_buf, next_buf, prev_buf,
           small_sem, load_sem, next_sem, turn_sem, count_sem, gather_send, gather_recv, own_sem):
    f32 = jnp.float32
    bf16 = jnp.bfloat16
    feed = lax.axis_index("feed")
    tm = lax.axis_index("tm")

    z_hi, y = feed // 8, lax.rem(feed, 8)
    after, before = lax.rem(tm + 1, NT), lax.rem(tm + NT - 1, NT)

    def feed_at(dz, dy):
        return lax.rem(z_hi + dz, 4) * 8 + lax.rem(y + dy, 8)

    barrier = pltpu.get_barrier_semaphore()

    def greet(feed_to, tm_to):
        pl.semaphore_signal(barrier, inc=1, device_id={"feed": feed_to, "tm": tm_to}, device_id_type=MESH)

    smalls = [
        pltpu.make_async_copy(src, dst, small_sem.at[n])
        for n, (src, dst) in enumerate(((order_hbm, order), (coef_hbm, coef), (flags_hbm, flags)))
    ]
    for small in smalls:
        small.start()
    loads = []
    for f in (7, 6, 5, 4, 3, 2, 1, 0):
        load = pltpu.make_async_copy(
            volt.at[:, pl.ds(f * FRAME, FRAME)], frames.at[pl.ds(f * INPUTS, INPUTS), :], load_sem.at[f]
        )
        load.start()
        loads.append(load)
    for step in FAR:
        greet(feed_at(*step), before)
        greet(feed_at(*step), tm)
    for step in range(1, NT):
        greet(feed, lax.rem(tm + step, NT))

    for small in smalls:
        small.wait()

    c_row = lax.broadcasted_iota(jnp.int32, (NCHAN, 2 * NF), 0)
    k_col = lax.broadcasted_iota(jnp.int32, (NCHAN, 2 * NF), 1)
    pick = k_col == 2 * (c_row & (NF - 1)) + (c_row >> 6)
    order_f = order[...].astype(f32)
    place = jnp.sum(jnp.where(pick, order_f, 0.0), axis=1, keepdims=True)
    chan_of = place.astype(jnp.int32)
    freq = jnp.broadcast_to(chan_of + CHAN0, (NCHAN, 128))
    lane = lax.broadcasted_iota(jnp.int32, (NCHAN, 128), 1)
    part = (lax.broadcasted_iota(jnp.int32, (NCHAN, 128), 0) >> 5) & 1
    phase0 = freq * lane + part * (FRAME // 4)
    phase_step = freq * 128
    scale = (TAPS * FRAME / 2.0) ** (-0.5)

    def table_block(a, phase):
        cols = pl.ds(pl.multiple_of(a * 128, 128), 128)
        dist = jnp.abs((phase & (FRAME - 1)) - FRAME // 2).astype(f32)
        z = dist * (4.0 / FRAME) - 1.0
        z2 = z * z
        trig = jnp.full_like(z, SINE[-1])
        for term in SINE[-2::-1]:
            trig = trig * z2 + term
        trig = trig * z
        for t in range(TAPS):
            table[pl.ds(t * NCHAN, NCHAN), cols] = (trig * (coef[pl.ds(t, 1), cols] * scale)).astype(bf16)
        return phase + phase_step

    lax.fori_loop(0, FRAME // 128, table_block, phase0)

    hot = (lax.broadcasted_iota(jnp.int32, (NCHAN, 2 * NF), 1) == chan_of).astype(bf16)
    nt = (((1,), (1,)), ((), ()))
    good = lax.dot_general(flags[...].astype(f32).astype(bf16), hot, nt, preferred_element_type=f32)
    local = jnp.sum(good, axis=0, keepdims=True)
    lane1 = lax.broadcasted_iota(jnp.int32, (1, NCHAN), 1)
    counts = [
        jnp.sum(jnp.where(lane1 == feed + kl * 2 * NF, local, 0.0), axis=1, keepdims=True) for kl in range(2)
    ]
    sub8 = lax.broadcasted_iota(jnp.int32, (8, 128), 0)
    count_buf[tm] = jnp.where(sub8 < 4, counts[0], counts[1])

    for load in loads:
        load.wait()
    prod[...] = lax.dot_general(frames[...], table[...], nt, preferred_element_type=f32)

    def term(f, t):
        return prod[pl.ds(f * INPUTS, INPUTS), pl.ds(t * NCHAN, NCHAN)]

    def partial(s):
        terms = [term(s - 3 + t, t) for t in range(TAPS) if 0 <= s - 3 + t < FRAMES]
        total = terms[0]
        for other in terms[1:]:
            total = total + other
        return total

    for j in range(2):
        last = partial(FRAMES + 2 * j + 1) if j == 0 else jnp.zeros((INPUTS, NCHAN), f32)
        turned = jnp.concatenate([partial(FRAMES + 2 * j), last], axis=0).T
        for q in range(4):
            next_buf[:, (q // 2) * 4 + (q % 2) * 2 + j, :] = turned[q * NF : (q + 1) * NF, :]
    for j in range(4):
        turned = jnp.concatenate([partial(2 * j), partial(2 * j + 1)], axis=0).T
        for q in range(4):
            rows[:, (q // 2) * 8 + (j // 2) * 4 + (q % 2) * 2 + j % 2, :] = turned[q * NF : (q + 1) * NF, :]
    send_buf[...] = rows[...].astype(bf16)

    pl.semaphore_wait(barrier, 2 * (NF - 1) + NT - 1)

    def send_next(peer):
        pltpu.make_async_remote_copy(
            src_ref=next_buf.at[peer], dst_ref=prev_buf.at[feed],
            send_sem=next_sem.at[0], recv_sem=next_sem.at[1],
            device_id={"feed": peer, "tm": after}, device_id_type=MESH,
        ).start()

    for step in FAR:
        peer = feed_at(*step)
        send_next(peer)
        pltpu.make_async_remote_copy(
            src_ref=send_buf.at[peer], dst_ref=recv_buf.at[feed],
            send_sem=turn_sem.at[0], recv_sem=turn_sem.at[1],
            device_id={"feed": peer, "tm": tm}, device_id_type=MESH,
        ).start()
    send_next(feed)
    own = pltpu.make_async_copy(send_buf.at[feed], recv_buf.at[feed], own_sem.at[0])
    own.start()

    def send_count(step, carry):
        pltpu.make_async_remote_copy(
            src_ref=count_buf.at[tm], dst_ref=count_buf.at[tm],
            send_sem=count_sem.at[0], recv_sem=count_sem.at[1],
            device_id={"tm": lax.rem(tm + step, NT)}, device_id_type=MESH,
        ).start()
        return carry

    lax.fori_loop(1, NT, send_count, 0)

    row = lax.broadcasted_iota(jnp.int32, (32, FRAMES), 0)
    spec = (row & 1) * 2 + ((row >> 2) & 1) * 4 + (row >> 4)
    match = (spec == lax.broadcasted_iota(jnp.int32, (32, FRAMES), 1)).astype(bf16)
    every_flag = jnp.dot(match, good.astype(bf16), preferred_element_type=f32)
    row = lax.broadcasted_iota(jnp.int32, (32, NCHAN), 0)
    mine = lax.broadcasted_iota(jnp.int32, (32, NCHAN), 1) == feed + ((row >> 3) & 1) * 2 * NF
    clean = jnp.sum(jnp.where(mine, every_flag, 0.0), axis=1, keepdims=True)

    own.wait()
    others = recv_buf.at[pl.ds(0, NF - 1)]
    pltpu.make_async_copy(others, others, turn_sem.at[1]).wait()
    pltpu.make_async_copy(prev_buf, prev_buf, next_sem.at[1]).wait()

    low = lax.broadcasted_iota(jnp.int32, (16, 128), 1) < INPUTS
    top = jnp.logical_and(lax.broadcasted_iota(jnp.int32, (8, 128), 0) < 4, tm > 0)

    def received(f):
        prev = prev_buf[f]
        both = jnp.concatenate([jnp.where(top, prev, 0.0), jnp.where(top, pltpu.roll(prev, 4, 0), 0.0)], axis=0)
        return recv_buf[f].astype(f32) + both

    for g in range(NF // 2):
        one = received(2 * g)
        two = received(2 * g + 1)
        first = jnp.where(low, one, pltpu.roll(two, INPUTS, 1)) * clean[:16]
        second = jnp.where(low, pltpu.roll(one, INPUTS, 1), two) * clean[16:]
        for kl in range(2):
            block = jnp.concatenate([first[kl * 8 : kl * 8 + 8], second[kl * 8 : kl * 8 + 8]], axis=0)
            full[kl, tm, :, pl.ds(g * 128, 128)] = block.astype(bf16)

    x, zed, core = tm // 4, lax.rem(tm // 2, 2), lax.rem(tm, 2)

    def at(dx, dz, dc):
        return lax.rem(x + dx, 4) * 4 + lax.rem(zed + dz, 2) * 2 + lax.rem(core + dc, 2)

    targets = {"sib": at(0, 0, 1), "zed": at(0, 1, 0), "right": at(1, 0, 0), "left": at(3, 0, 0)}
    blocks = {"own": (0, 0), "z": (0, 1), "l": (3, 0), "r": (1, 0), "lz": (3, 1), "rz": (1, 1), "o": (2, 0), "oz": (2, 1)}
    moves = {"sib": (0, 0, 1), "zed": (0, 1, 0), "right": (3, 0, 0), "left": (1, 0, 0)}
    lanes = {"all": pl.ds(0, COLS), "lo": pl.ds(0, HALF), "hi": pl.ds(HALF, HALF)}

    def view(kl, index, which):
        return full.at[kl, index, :, lanes[which]]

    def send(kl, event):
        block, which, target = GATHER[event]
        ref = view(kl, at(*blocks[block], 0), which)
        copy = pltpu.make_async_remote_copy(
            src_ref=ref, dst_ref=ref,
            send_sem=gather_send.at[kl, event], recv_sem=gather_recv.at[kl, event],
            device_id={"tm": targets[target]}, device_id_type=MESH,
        )
        copy.start()

    def arrived(kl, event):
        block, which, target = GATHER[event]
        dx, dz = blocks[block]
        mx, mz, mc = moves[target]
        ref = view(kl, at((dx + mx) % 4, (dz + mz) % 2, mc), which)
        pltpu.make_async_copy(ref, ref, gather_recv.at[kl, event]).wait()

    def sent(kl, event):
        block, which, _ = GATHER[event]
        ref = view(kl, at(*blocks[block], 0), which)
        pltpu.make_async_copy(ref, ref, gather_send.at[kl, event]).wait()

    def relay(kl, event, *following):
        arrived(kl, event)
        for after in following:
            send(kl, after)

    for kl in range(2):
        for event in (2, 3, 1, 0):
            send(kl, event)
    for kl in range(2):
        relay(kl, 1, 5, 6, 4)
        relay(kl, 2, 8, 7)
        relay(kl, 3, 10, 9)
    for kl in range(2):
        relay(kl, 5, 12, 11)
        relay(kl, 6, 14, 13)

    for kl in range(2):
        relay(kl, 8, 15)
        relay(kl, 10, 16)
        relay(kl, 12, 17)
        relay(kl, 14, 18)
    every = count_buf.at[pl.ds(0, NT - 1)]
    pltpu.make_async_copy(every, every, count_sem.at[1]).wait()
    for kl in range(2):
        for event in (0, 4, 7, 9, 11, 13, 15, 16, 17, 18):
            arrived(kl, event)
    pltpu.make_async_copy(every, every, count_sem.at[0]).wait()
    gone = send_buf.at[pl.ds(0, NF - 1)]
    pltpu.make_async_copy(gone, gone, turn_sem.at[0]).wait()
    pltpu.make_async_copy(next_buf, next_buf, next_sem.at[0]).wait()
    for kl in range(2):
        for event in range(EVENTS):
            sent(kl, event)


def correlate(full, count_buf, out_re, out_im, stage_re, stage_im, store_sem):
    f32 = jnp.float32
    bf16 = jnp.bfloat16
    tm = lax.axis_index("tm")
    inverse = 1.0 / jnp.maximum(jnp.sum(count_buf[...], axis=0), 1.0)
    mine = pl.ds(pl.multiple_of(tm * 128, 128), 128)
    odd = (lax.broadcasted_iota(jnp.int32, (256, 128), 0) & 2) > 0
    stores = []
    for kl in range(2):
        left = full[kl, :, :, mine].reshape(256, 128).astype(f32)
        swapped = jnp.where(odd, -pltpu.roll(left, 2, 0), pltpu.roll(left, 254, 0))
        both = jnp.concatenate([left.T, swapped.T], axis=0).astype(bf16)
        factor = inverse[4 * kl : 4 * kl + 1, 0:1]
        for n in range(COLS // WIDE):
            cols = pl.ds(n * WIDE, WIDE)
            right = full[kl, :, :, cols].reshape(256, WIDE)
            result = jnp.dot(both, right, preferred_element_type=f32) * factor
            stage_re[kl, :, cols] = result[:128].astype(bf16)
            stage_im[kl, :, cols] = result[128:].astype(bf16)
            for part, (stage, out) in enumerate(((stage_re, out_re), (stage_im, out_im))):
                store = pltpu.make_async_copy(stage.at[kl, :, cols], out.at[kl, :, cols], store_sem.at[kl, n, part])
                store.start()
                stores.append(store)
    for store in stores:
        store.wait()


def body(voltages, pfb_coeffs, flags, channel_order):
    hbm = pl.BlockSpec(memory_space=pltpu.HBM)
    vmem = pl.BlockSpec(memory_space=pltpu.VMEM)
    bf16 = jnp.bfloat16
    f32 = jnp.float32
    dma = pltpu.SemaphoreType.DMA
    args = (voltages, pfb_coeffs, flags, channel_order.reshape(1, -1))
    full, counts = pl.pallas_call(
        kernel,
        out_shape=(jax.ShapeDtypeStruct((2, NT, 16, COLS), bf16), jax.ShapeDtypeStruct((NT, 8, 128), f32)),
        in_specs=[hbm] * 4,
        out_specs=(vmem, vmem),
        scratch_shapes=[
            pltpu.VMEM((TAPS, FRAME), f32),
            pltpu.VMEM((FRAMES, 2 * NF), jnp.int32),
            pltpu.VMEM((1, 2 * NF), jnp.int32),
            pltpu.VMEM((FRAMES * INPUTS, FRAME), bf16),
            pltpu.VMEM((TAPS * NCHAN, FRAME), bf16),
            pltpu.VMEM((FRAMES * INPUTS, TAPS * NCHAN), f32),
            pltpu.VMEM((NF, 16, 128), f32),
            pltpu.VMEM((NF, 16, 128), bf16),
            pltpu.VMEM((NF, 16, 128), bf16),
            pltpu.VMEM((NF, 8, 128), f32),
            pltpu.VMEM((NF, 8, 128), f32),
            dma((3,)),
            dma((FRAMES,)),
            dma((2,)),
            dma((2,)),
            dma((2,)),
            dma((2, EVENTS)),
            dma((2, EVENTS)),
            dma((1,)),
        ],
        compiler_params=pltpu.CompilerParams(
            collective_id=0, has_side_effects=True, vmem_limit_bytes=24 * 1024 * 1024
        ),
        name="channelize_gather",
    )(*(pltpu.with_memory_space_constraint(a, pltpu.HBM) for a in args))
    out = jax.ShapeDtypeStruct((2, 128, COLS), bf16)
    return pl.pallas_call(
        correlate,
        out_shape=(out, out),
        in_specs=[vmem, vmem],
        out_specs=(hbm, hbm),
        scratch_shapes=[
            pltpu.VMEM((2, 128, COLS), bf16),
            pltpu.VMEM((2, 128, COLS), bf16),
            dma((2, COLS // WIDE, 2)),
        ],
        compiler_params=pltpu.CompilerParams(vmem_limit_bytes=24 * 1024 * 1024),
        name="correlate",
    )(full, counts)


def solution(mesh):
    return jax.shard_map(
        body,
        mesh=mesh,
        in_specs=(P("feed", "tm"), P(), P("tm", None), P()),
        out_specs=(P("feed", "tm", None), P("feed", "tm", None)),
        check_vma=False,
    )
```

```python
import functools
import math

import jax
import jax.numpy as jnp
from jax import lax
from jax.experimental import pallas as pl
from jax.experimental.pallas import tpu as pltpu
from jax.sharding import PartitionSpec as P

CHAN0 = 448
NF = 32
NT = 16
INPUTS = 64
FRAMES = 8
TAPS = 4
FRAME = 2048
COLS = 2048
HALF = COLS // 2
WIDE = 512
NCHAN = 4 * NF
MESH = pl.DeviceIdType.MESH
SINE = [(math.pi / 2) ** n / math.factorial(n) * (-1) ** (n // 2) for n in (1, 3, 5, 7, 9, 11)]

BOTH = (0, 1)
GATHER = {
    "own0z": ("own", (0,), "all", "zed", ()),
    "own1r": ("own", (1,), "all", "right", ()),
    "own1l": ("own", (1,), "all", "left", ()),
    "own1o": ("own", (1,), "all", "over", ()),
    "own1z": ("own", (1,), "all", "zed", ()),
    "own0r": ("own", (0,), "all", "right", ()),
    "own0l": ("own", (0,), "all", "left", ()),
    "owns": ("own", BOTH, "all", "sib", ()),
    "z0r": ("z", (0,), "all", "right", ("own0z",)),
    "z0l": ("z", (0,), "all", "left", ("own0z",)),
    "z0o": ("z", (0,), "all", "over", ("own0z",)),
    "l1z": ("l", (1,), "all", "zed", ("own1r",)),
    "r1z": ("r", (1,), "all", "zed", ("own1l",)),
    "o1z": ("o", (1,), "all", "zed", ("own1o",)),
    "l0r": ("l", (0,), "lo", "right", ("own0r",)),
    "r0l": ("r", (0,), "hi", "left", ("own0l",)),
    "zs": ("z", BOTH, "all", "sib", ("own0z", "own1z")),
    "ls": ("l", BOTH, "all", "sib", ("own1r", "own0r")),
    "rs": ("r", BOTH, "all", "sib", ("own1l", "own0l")),
    "lzs": ("lz", BOTH, "all", "sib", ("z0r", "l1z")),
    "rzs": ("rz", BOTH, "all", "sib", ("z0l", "r1z")),
    "os": ("o", BOTH, "all", "sib", ("own1o", "l0r", "r0l")),
    "ozs": ("oz", BOTH, "all", "sib", ("z0o", "o1z")),
}
EVENTS = len(GATHER)
ORDER = ("own0z", "own1r", "own1l", "own1z", "own1o", "own0r", "own0l", "z0r", "l1z", "z0l", "r1z", "l0r", "r0l", "z0o", "o1z")

FAR = sorted(
    ((dz, dy) for dz in range(4) for dy in range(8) if dz or dy),
    key=lambda step: -(2 * min(step[0], 4 - step[0]) + min(step[1], 8 - step[1])),
)


def kernel(volt, coef_hbm, flags_hbm, order_hbm, full, count_buf, coef, flags, order, frames, table, prod,
           rows, send_buf, recv_buf, next_buf, prev_buf,
           small_sem, load_sem, next_sem, turn_sem, count_sem, gather_send, gather_recv, own_sem):
    f32 = jnp.float32
    bf16 = jnp.bfloat16
    feed = lax.axis_index("feed")
    tm = lax.axis_index("tm")

    z_hi, y = feed // 8, lax.rem(feed, 8)
    after = lax.rem(tm + 1, NT)

    def feed_at(dz, dy):
        return lax.rem(z_hi + dz, 4) * 8 + lax.rem(y + dy, 8)

    barrier = pltpu.get_barrier_semaphore()

    def greet(feed_to, tm_to):
        pl.semaphore_signal(barrier, inc=1, device_id={"feed": feed_to, "tm": tm_to}, device_id_type=MESH)

    smalls = [
        pltpu.make_async_copy(src, dst, small_sem.at[n])
        for n, (src, dst) in enumerate(((order_hbm, order), (coef_hbm, coef), (flags_hbm, flags)))
    ]
    for small in smalls:
        small.start()
    loads = []
    for f in (7, 6, 5, 4, 3, 2, 1, 0):
        load = pltpu.make_async_copy(
            volt.at[:, pl.ds(f * FRAME, FRAME)], frames.at[pl.ds(f * INPUTS, INPUTS), :], load_sem.at[f]
        )
        load.start()
        loads.append(load)
    for step in FAR:
        greet(feed_at(*step), tm)
    for step in range(1, NT):
        greet(feed, lax.rem(tm + step, NT))

    for small in smalls:
        small.wait()

    c_row = lax.broadcasted_iota(jnp.int32, (NCHAN, 2 * NF), 0)
    k_col = lax.broadcasted_iota(jnp.int32, (NCHAN, 2 * NF), 1)
    pick = k_col == 2 * (c_row & (NF - 1)) + (c_row >> 6)
    order_f = order[...].astype(f32)
    place = jnp.sum(jnp.where(pick, order_f, 0.0), axis=1, keepdims=True)
    chan_of = place.astype(jnp.int32)
    freq = jnp.broadcast_to(chan_of + CHAN0, (NCHAN, 128))
    lane = lax.broadcasted_iota(jnp.int32, (NCHAN, 128), 1)
    part = (lax.broadcasted_iota(jnp.int32, (NCHAN, 128), 0) >> 5) & 1
    phase0 = freq * lane + part * (FRAME // 4)
    phase_step = freq * 128
    scale = (TAPS * FRAME / 2.0) ** (-0.5)

    def table_block(a, phase):
        cols = pl.ds(pl.multiple_of(a * 128, 128), 128)
        dist = jnp.abs((phase & (FRAME - 1)) - FRAME // 2).astype(f32)
        z = dist * (4.0 / FRAME) - 1.0
        z2 = z * z
        trig = jnp.full_like(z, SINE[-1])
        for term in SINE[-2::-1]:
            trig = trig * z2 + term
        trig = trig * z
        for t in range(TAPS):
            table[pl.ds(t * NCHAN, NCHAN), cols] = (trig * (coef[pl.ds(t, 1), cols] * scale)).astype(bf16)
        return phase + phase_step

    lax.fori_loop(0, FRAME // 128, table_block, phase0)

    hot = (lax.broadcasted_iota(jnp.int32, (NCHAN, 2 * NF), 1) == chan_of).astype(bf16)
    nt = (((1,), (1,)), ((), ()))
    good = lax.dot_general(flags[...].astype(f32).astype(bf16), hot, nt, preferred_element_type=f32)
    local = jnp.sum(good, axis=0, keepdims=True)
    lane1 = lax.broadcasted_iota(jnp.int32, (1, NCHAN), 1)
    counts = [
        jnp.sum(jnp.where(lane1 == feed + kl * 2 * NF, local, 0.0), axis=1, keepdims=True) for kl in range(2)
    ]
    sub8 = lax.broadcasted_iota(jnp.int32, (8, 128), 0)
    count_buf[tm] = jnp.where(sub8 < 4, counts[0], counts[1])

    for load in loads[:4]:
        load.wait()
    prod[pl.ds(256, 256), :] = lax.dot_general(
        frames[pl.ds(256, 256), :], table[...], nt, preferred_element_type=f32
    )

    def term(f, t):
        return prod[pl.ds(f * INPUTS, INPUTS), pl.ds(t * NCHAN, NCHAN)]

    def partial(s):
        terms = [term(s - 3 + t, t) for t in range(TAPS) if 0 <= s - 3 + t < FRAMES]
        total = terms[0]
        for other in terms[1:]:
            total = total + other
        return total

    for s in range(3):
        next_buf[pl.ds(s * INPUTS, INPUTS), :] = partial(FRAMES + s).astype(next_buf.dtype)
    pl.semaphore_wait(barrier, NF - 1 + NT - 1)
    halo = pltpu.make_async_remote_copy(
        src_ref=next_buf, dst_ref=prev_buf, send_sem=next_sem.at[0], recv_sem=next_sem.at[1],
        device_id={"tm": after}, device_id_type=MESH,
    )
    halo.start()
    for load in loads[4:]:
        load.wait()
    prod[pl.ds(0, 256), :] = lax.dot_general(
        frames[pl.ds(0, 256), :], table[...], nt, preferred_element_type=f32
    )

    def total(s):
        value = partial(s)
        if s < 3:
            value = value + jnp.where(tm > 0, prev_buf[pl.ds(s * INPUTS, INPUTS), :].astype(f32), 0.0)
        return value

    def turn(j):
        turned = jnp.concatenate([total(2 * j), total(2 * j + 1)], axis=0).T
        for q in range(4):
            rows[:, (q // 2) * 8 + (j // 2) * 4 + (q % 2) * 2 + j % 2, :] = turned[q * NF : (q + 1) * NF, :]

    turn(3)
    turn(2)
    halo.wait_recv()
    turn(1)
    turn(0)
    send_buf[...] = rows[...].astype(bf16)

    for step in FAR:
        peer = feed_at(*step)
        pltpu.make_async_remote_copy(
            src_ref=send_buf.at[peer], dst_ref=recv_buf.at[feed],
            send_sem=turn_sem.at[0], recv_sem=turn_sem.at[1],
            device_id={"feed": peer, "tm": tm}, device_id_type=MESH,
        ).start()
    own = pltpu.make_async_copy(send_buf.at[feed], recv_buf.at[feed], own_sem.at[0])
    own.start()

    def send_count(step, carry):
        pltpu.make_async_remote_copy(
            src_ref=count_buf.at[tm], dst_ref=count_buf.at[tm],
            send_sem=count_sem.at[0], recv_sem=count_sem.at[1],
            device_id={"tm": lax.rem(tm + step, NT)}, device_id_type=MESH,
        ).start()
        return carry

    lax.fori_loop(1, NT, send_count, 0)

    row = lax.broadcasted_iota(jnp.int32, (32, FRAMES), 0)
    spec = (row & 1) * 2 + ((row >> 2) & 1) * 4 + (row >> 4)
    match = (spec == lax.broadcasted_iota(jnp.int32, (32, FRAMES), 1)).astype(bf16)
    every_flag = jnp.dot(match, good.astype(bf16), preferred_element_type=f32)
    row = lax.broadcasted_iota(jnp.int32, (32, NCHAN), 0)
    mine = lax.broadcasted_iota(jnp.int32, (32, NCHAN), 1) == feed + ((row >> 3) & 1) * 2 * NF
    clean = jnp.sum(jnp.where(mine, every_flag, 0.0), axis=1, keepdims=True)

    own.wait()
    others = recv_buf.at[pl.ds(0, NF - 1)]
    pltpu.make_async_copy(others, others, turn_sem.at[1]).wait()

    low = lax.broadcasted_iota(jnp.int32, (16, 128), 1) < INPUTS
    for g in range(NF // 2):
        one = recv_buf[2 * g].astype(f32)
        two = recv_buf[2 * g + 1].astype(f32)
        first = jnp.where(low, one, pltpu.roll(two, INPUTS, 1)) * clean[:16]
        second = jnp.where(low, pltpu.roll(one, INPUTS, 1), two) * clean[16:]
        for kl in range(2):
            block = jnp.concatenate([first[kl * 8 : kl * 8 + 8], second[kl * 8 : kl * 8 + 8]], axis=0)
            full[kl, tm, :, pl.ds(g * 128, 128)] = block.astype(bf16)

    x, zed, core = tm // 4, lax.rem(tm // 2, 2), lax.rem(tm, 2)

    def at(dx, dz, dc):
        return lax.rem(x + dx, 4) * 4 + lax.rem(zed + dz, 2) * 2 + lax.rem(core + dc, 2)

    targets = {"sib": at(0, 0, 1), "zed": at(0, 1, 0), "right": at(1, 0, 0), "left": at(3, 0, 0), "over": at(2, 0, 0),
               "rightz": at(1, 1, 0), "leftz": at(3, 1, 0), "overz": at(2, 1, 0)}
    blocks = {"own": (0, 0), "z": (0, 1), "l": (3, 0), "r": (1, 0), "lz": (3, 1), "rz": (1, 1), "o": (2, 0), "oz": (2, 1)}
    moves = {"sib": (0, 0, 1), "zed": (0, 1, 0), "right": (3, 0, 0), "left": (1, 0, 0), "over": (2, 0, 0),
             "rightz": (3, 1, 0), "leftz": (1, 1, 0), "overz": (2, 1, 0)}
    lanes = {"all": pl.ds(0, COLS), "lo": pl.ds(0, HALF), "hi": pl.ds(HALF, HALF)}
    numbers = {name: n for n, name in enumerate(GATHER)}

    def view(index, chans, which):
        return full.at[pl.ds(chans[0], len(chans)), index, :, lanes[which]]

    def send(name):
        block, chans, which, target, _ = GATHER[name]
        ref = view(at(*blocks[block], 0), chans, which)
        pltpu.make_async_remote_copy(
            src_ref=ref, dst_ref=ref,
            send_sem=gather_send.at[numbers[name]], recv_sem=gather_recv.at[numbers[name]],
            device_id={"tm": targets[target]}, device_id_type=MESH,
        ).start()

    def arrived(name):
        block, chans, which, target, _ = GATHER[name]
        dx, dz = blocks[block]
        mx, mz, mc = moves[target]
        ref = view(at((dx + mx) % 4, (dz + mz) % 2, mc), chans, which)
        pltpu.make_async_copy(ref, ref, gather_recv.at[numbers[name]]).wait()

    def sent(name):
        block, chans, which, _, _ = GATHER[name]
        ref = view(at(*blocks[block], 0), chans, which)
        pltpu.make_async_copy(ref, ref, gather_send.at[numbers[name]]).wait()

    here = set()
    for name in GATHER:
        if not GATHER[name][4]:
            send(name)
    for name in ORDER:
        arrived(name)
        here.add(name)
        for later in GATHER:
            if name in GATHER[later][4] and here.issuperset(GATHER[later][4]):
                send(later)
    every = count_buf.at[pl.ds(0, NT - 1)]
    pltpu.make_async_copy(every, every, count_sem.at[1]).wait()
    for name in GATHER:
        if name not in ORDER:
            arrived(name)
    pltpu.make_async_copy(every, every, count_sem.at[0]).wait()
    gone = send_buf.at[pl.ds(0, NF - 1)]
    pltpu.make_async_copy(gone, gone, turn_sem.at[0]).wait()
    halo.wait_send()
    for name in GATHER:
        sent(name)


def correlate(full, count_buf, out_re, out_im, stage_re, stage_im, store_sem):
    f32 = jnp.float32
    bf16 = jnp.bfloat16
    tm = lax.axis_index("tm")
    inverse = 1.0 / jnp.maximum(jnp.sum(count_buf[...], axis=0), 1.0)
    mine = pl.ds(pl.multiple_of(tm * 128, 128), 128)
    odd = (lax.broadcasted_iota(jnp.int32, (256, 128), 0) & 2) > 0
    stores = []
    for kl in range(2):
        left = full[kl, :, :, mine].reshape(256, 128).astype(f32)
        swapped = jnp.where(odd, -pltpu.roll(left, 2, 0), pltpu.roll(left, 254, 0))
        both = jnp.concatenate([left.T, swapped.T], axis=0).astype(bf16)
        factor = inverse[4 * kl : 4 * kl + 1, 0:1]
        for n in range(COLS // WIDE):
            cols = pl.ds(n * WIDE, WIDE)
            right = full[kl, :, :, cols].reshape(256, WIDE)
            result = jnp.dot(both, right, preferred_element_type=f32) * factor
            stage_re[kl, :, cols] = result[:128].astype(bf16)
            stage_im[kl, :, cols] = result[128:].astype(bf16)
            for part, (stage, out) in enumerate(((stage_re, out_re), (stage_im, out_im))):
                store = pltpu.make_async_copy(stage.at[kl, :, cols], out.at[kl, :, cols], store_sem.at[kl, n, part])
                store.start()
                stores.append(store)
    for store in stores:
        store.wait()


def body(voltages, pfb_coeffs, flags, channel_order):
    hbm = pl.BlockSpec(memory_space=pltpu.HBM)
    vmem = pl.BlockSpec(memory_space=pltpu.VMEM)
    bf16 = jnp.bfloat16
    f32 = jnp.float32
    dma = pltpu.SemaphoreType.DMA
    args = (voltages, pfb_coeffs, flags, channel_order.reshape(1, -1))
    full, counts = pl.pallas_call(
        kernel,
        out_shape=(jax.ShapeDtypeStruct((2, NT, 16, COLS), bf16), jax.ShapeDtypeStruct((NT, 8, 128), f32)),
        in_specs=[hbm] * 4,
        out_specs=(vmem, vmem),
        scratch_shapes=[
            pltpu.VMEM((TAPS, FRAME), f32),
            pltpu.VMEM((FRAMES, 2 * NF), jnp.int32),
            pltpu.VMEM((1, 2 * NF), jnp.int32),
            pltpu.VMEM((FRAMES * INPUTS, FRAME), bf16),
            pltpu.VMEM((TAPS * NCHAN, FRAME), bf16),
            pltpu.VMEM((FRAMES * INPUTS, TAPS * NCHAN), f32),
            pltpu.VMEM((NF, 16, 128), f32),
            pltpu.VMEM((NF, 16, 128), bf16),
            pltpu.VMEM((NF, 16, 128), bf16),
            pltpu.VMEM((3 * INPUTS, NCHAN), f32),
            pltpu.VMEM((3 * INPUTS, NCHAN), f32),
            dma((3,)),
            dma((FRAMES,)),
            dma((2,)),
            dma((2,)),
            dma((2,)),
            dma((EVENTS,)),
            dma((EVENTS,)),
            dma((1,)),
        ],
        compiler_params=pltpu.CompilerParams(
            collective_id=0, has_side_effects=True, vmem_limit_bytes=24 * 1024 * 1024
        ),
        name="channelize_gather",
    )(*(pltpu.with_memory_space_constraint(a, pltpu.HBM) for a in args))
    out = jax.ShapeDtypeStruct((2, 128, COLS), bf16)
    return pl.pallas_call(
        correlate,
        out_shape=(out, out),
        in_specs=[vmem, vmem],
        out_specs=(hbm, hbm),
        scratch_shapes=[
            pltpu.VMEM((2, 128, COLS), bf16),
            pltpu.VMEM((2, 128, COLS), bf16),
            dma((2, COLS // WIDE, 2)),
        ],
        compiler_params=pltpu.CompilerParams(vmem_limit_bytes=24 * 1024 * 1024),
        name="correlate",
    )(full, counts)


def solution(mesh):
    return jax.shard_map(
        body,
        mesh=mesh,
        in_specs=(P("feed", "tm"), P(), P("tm", None), P()),
        out_specs=(P("feed", "tm", None), P("feed", "tm", None)),
        check_vma=False,
    )
```

```python
import functools
import math

import jax
import jax.numpy as jnp
from jax import lax
from jax.experimental import pallas as pl
from jax.experimental.pallas import tpu as pltpu
from jax.sharding import PartitionSpec as P

CHAN0 = 448
NF = 32
NT = 16
INPUTS = 64
FRAMES = 8
TAPS = 4
FRAME = 2048
COLS = 2048
HALF = COLS // 2
WIDE = 512
NCHAN = 4 * NF
MESH = pl.DeviceIdType.MESH
SINE = [(math.pi / 2) ** n / math.factorial(n) * (-1) ** (n // 2) for n in (1, 3, 5, 7, 9, 11)]

BOTH = (0, 1)
GATHER = {
    "own0z": ("own", (0,), "all", "zed", ()),
    "own1r": ("own", (1,), "all", "right", ()),
    "own1l": ("own", (1,), "all", "left", ()),
    "own1o": ("own", (1,), "all", "over", ()),
    "own1z": ("own", (1,), "all", "zed", ()),
    "own0r": ("own", (0,), "all", "right", ()),
    "own0l": ("own", (0,), "all", "left", ()),
    "owns": ("own", BOTH, "all", "sib", ()),
    "z0r": ("z", (0,), "all", "right", ("own0z",)),
    "z0l": ("z", (0,), "all", "left", ("own0z",)),
    "z0o": ("z", (0,), "all", "over", ("own0z",)),
    "l1z": ("l", (1,), "all", "zed", ("own1r",)),
    "r1z": ("r", (1,), "all", "zed", ("own1l",)),
    "o1z": ("o", (1,), "all", "zed", ("own1o",)),
    "l0r": ("l", (0,), "lo", "right", ("own0r",)),
    "r0l": ("r", (0,), "hi", "left", ("own0l",)),
    "zs": ("z", BOTH, "all", "sib", ("own0z", "own1z")),
    "ls": ("l", BOTH, "all", "sib", ("own1r", "own0r")),
    "rs": ("r", BOTH, "all", "sib", ("own1l", "own0l")),
    "lzs": ("lz", BOTH, "all", "sib", ("z0r", "l1z")),
    "rzs": ("rz", BOTH, "all", "sib", ("z0l", "r1z")),
    "os": ("o", BOTH, "all", "sib", ("own1o", "l0r", "r0l")),
    "ozs": ("oz", BOTH, "all", "sib", ("z0o", "o1z")),
}
EVENTS = len(GATHER)
PLACE = {"own": 0, "r": 1, "o": 2, "l": 3, "z": 4, "rz": 5, "oz": 6, "lz": 7}
ORDER = ("own0z", "own1r", "own1l", "own1z", "own1o", "own0r", "own0l", "z0r", "l1z", "z0l", "r1z", "l0r", "r0l", "z0o", "o1z")

FAR = sorted(
    ((dz, dy) for dz in range(4) for dy in range(8) if dz or dy),
    key=lambda step: -(2 * min(step[0], 4 - step[0]) + min(step[1], 8 - step[1])),
)


def kernel(volt, coef_hbm, flags_hbm, order_hbm, full, count_buf, coef, flags, order, frames, table, prod,
           rows, send_buf, recv_buf, next_buf, prev_buf,
           small_sem, load_sem, next_sem, turn_sem, count_sem, gather_send, gather_recv, own_sem):
    f32 = jnp.float32
    bf16 = jnp.bfloat16
    feed = lax.axis_index("feed")
    tm = lax.axis_index("tm")

    z_hi, y = feed // 8, lax.rem(feed, 8)
    after = lax.rem(tm + 1, NT)

    def feed_at(dz, dy):
        return lax.rem(z_hi + dz, 4) * 8 + lax.rem(y + dy, 8)

    barrier = pltpu.get_barrier_semaphore()

    def greet(feed_to, tm_to):
        pl.semaphore_signal(barrier, inc=1, device_id={"feed": feed_to, "tm": tm_to}, device_id_type=MESH)

    for step in FAR[:8]:
        greet(feed_at(*step), tm)
    smalls = [
        pltpu.make_async_copy(src, dst, small_sem.at[n])
        for n, (src, dst) in enumerate(((order_hbm, order), (coef_hbm, coef), (flags_hbm, flags)))
    ]
    for small in smalls:
        small.start()
    loads = []
    for f in (7, 6, 5, 4, 3, 2, 1, 0):
        load = pltpu.make_async_copy(
            volt.at[:, pl.ds(f * FRAME, FRAME)], frames.at[pl.ds(f * INPUTS, INPUTS), :], load_sem.at[f]
        )
        load.start()
        loads.append(load)
    for step in FAR[8:]:
        greet(feed_at(*step), tm)
    for step in range(1, NT):
        greet(feed, lax.rem(tm + step, NT))

    for small in smalls:
        small.wait()

    c_row = lax.broadcasted_iota(jnp.int32, (NCHAN, 2 * NF), 0)
    k_col = lax.broadcasted_iota(jnp.int32, (NCHAN, 2 * NF), 1)
    pick = k_col == 2 * (c_row & (NF - 1)) + (c_row >> 6)
    order_f = order[...].astype(f32)
    place = jnp.sum(jnp.where(pick, order_f, 0.0), axis=1, keepdims=True)
    chan_of = place.astype(jnp.int32)
    freq = jnp.broadcast_to(chan_of + CHAN0, (NCHAN, 128))
    lane = lax.broadcasted_iota(jnp.int32, (NCHAN, 128), 1)
    part = (lax.broadcasted_iota(jnp.int32, (NCHAN, 128), 0) >> 5) & 1
    scale = (TAPS * FRAME / 2.0) ** (-0.5)

    def trig(phase):
        dist = jnp.abs((phase & (FRAME - 1)) - FRAME // 2).astype(f32)
        z = dist * (4.0 / FRAME) - 1.0
        z2 = z * z
        value = jnp.full_like(z, SINE[-1])
        for power in SINE[-2::-1]:
            value = value * z2 + power
        return value * z

    quarter = FRAME // 4
    first = trig(freq * lane + part * quarter)
    turn_cos = trig(freq * 128)
    turn_sin = trig(freq * 128 - quarter)
    signed = jnp.where(part == 0, turn_sin, -turn_sin)

    def table_block(a, value):
        cols = pl.ds(pl.multiple_of(a * 128, 128), 128)
        for t in range(TAPS):
            table[pl.ds(t * NCHAN, NCHAN), cols] = (value * (coef[pl.ds(t, 1), cols] * scale)).astype(bf16)
        swapped = jnp.concatenate([value[n * NF : (n + 1) * NF] for n in (1, 0, 3, 2)], axis=0)
        return value * turn_cos + swapped * signed

    lax.fori_loop(0, FRAME // 128, table_block, first)

    hot = (lax.broadcasted_iota(jnp.int32, (NCHAN, 2 * NF), 1) == chan_of).astype(bf16)
    nt = (((1,), (1,)), ((), ()))
    good = lax.dot_general(flags[...].astype(f32).astype(bf16), hot, nt, preferred_element_type=f32)
    local = jnp.sum(good, axis=0, keepdims=True)
    lane1 = lax.broadcasted_iota(jnp.int32, (1, NCHAN), 1)
    counts = [
        jnp.sum(jnp.where(lane1 == feed + kl * 2 * NF, local, 0.0), axis=1, keepdims=True) for kl in range(2)
    ]
    sub8 = lax.broadcasted_iota(jnp.int32, (8, 128), 0)
    count_buf[tm] = jnp.where(sub8 < 4, counts[0], counts[1])

    for load in loads[:4]:
        load.wait()
    prod[pl.ds(256, 256), :] = lax.dot_general(
        frames[pl.ds(256, 256), :], table[...], nt, preferred_element_type=f32
    )

    def term(f, t):
        return prod[pl.ds(f * INPUTS, INPUTS), pl.ds(t * NCHAN, NCHAN)]

    def partial(s):
        terms = [term(s - 3 + t, t) for t in range(TAPS) if 0 <= s - 3 + t < FRAMES]
        total = terms[0]
        for other in terms[1:]:
            total = total + other
        return total

    for s in range(3):
        next_buf[pl.ds(s * INPUTS, INPUTS), :] = partial(FRAMES + s).astype(next_buf.dtype)
    pl.semaphore_wait(barrier, NF - 1 + NT - 1)
    halo = pltpu.make_async_remote_copy(
        src_ref=next_buf, dst_ref=prev_buf, send_sem=next_sem.at[0], recv_sem=next_sem.at[1],
        device_id={"tm": after}, device_id_type=MESH,
    )
    @pl.when(tm < NT - 1)
    def _():
        halo.start()

    for load in loads[4:]:
        load.wait()
    prod[pl.ds(0, 256), :] = lax.dot_general(
        frames[pl.ds(0, 256), :], table[...], nt, preferred_element_type=f32
    )

    def total(s):
        value = partial(s)
        if s < 3:
            value = value + jnp.where(tm > 0, prev_buf[pl.ds(s * INPUTS, INPUTS), :].astype(f32), 0.0)
        return value

    def turn(j):
        turned = jnp.concatenate([total(2 * j), total(2 * j + 1)], axis=0).T
        for q in range(4):
            rows[:, (q // 2) * 8 + (j // 2) * 4 + (q % 2) * 2 + j % 2, :] = turned[q * NF : (q + 1) * NF, :]

    turn(3)
    turn(2)
    @pl.when(tm > 0)
    def _():
        halo.wait_recv()

    turn(1)
    turn(0)
    send_buf[...] = rows[...].astype(bf16)

    for step in FAR:
        peer = feed_at(*step)
        pltpu.make_async_remote_copy(
            src_ref=send_buf.at[peer], dst_ref=recv_buf.at[feed],
            send_sem=turn_sem.at[0], recv_sem=turn_sem.at[1],
            device_id={"feed": peer, "tm": tm}, device_id_type=MESH,
        ).start()
    own = pltpu.make_async_copy(send_buf.at[feed], recv_buf.at[feed], own_sem.at[0])
    own.start()

    def send_count(step, carry):
        pltpu.make_async_remote_copy(
            src_ref=count_buf.at[tm], dst_ref=count_buf.at[tm],
            send_sem=count_sem.at[0], recv_sem=count_sem.at[1],
            device_id={"tm": lax.rem(tm + step, NT)}, device_id_type=MESH,
        ).start()
        return carry

    lax.fori_loop(1, NT, send_count, 0)

    row = lax.broadcasted_iota(jnp.int32, (32, FRAMES), 0)
    spec = (row & 1) * 2 + ((row >> 2) & 1) * 4 + (row >> 4)
    match = (spec == lax.broadcasted_iota(jnp.int32, (32, FRAMES), 1)).astype(bf16)
    every_flag = jnp.dot(match, good.astype(bf16), preferred_element_type=f32)
    row = lax.broadcasted_iota(jnp.int32, (32, NCHAN), 0)
    mine = lax.broadcasted_iota(jnp.int32, (32, NCHAN), 1) == feed + ((row >> 3) & 1) * 2 * NF
    clean = jnp.sum(jnp.where(mine, every_flag, 0.0), axis=1, keepdims=True)

    own.wait()
    others = recv_buf.at[pl.ds(0, NF - 1)]
    pltpu.make_async_copy(others, others, turn_sem.at[1]).wait()

    low = lax.broadcasted_iota(jnp.int32, (16, 128), 1) < INPUTS
    for g in range(NF // 2):
        one = recv_buf[2 * g].astype(f32)
        two = recv_buf[2 * g + 1].astype(f32)
        first = jnp.where(low, one, pltpu.roll(two, INPUTS, 1)) * clean[:16]
        second = jnp.where(low, pltpu.roll(one, INPUTS, 1), two) * clean[16:]
        for kl in range(2):
            block = jnp.concatenate([first[kl * 8 : kl * 8 + 8], second[kl * 8 : kl * 8 + 8]], axis=0)
            full[kl, 0, :, pl.ds(g * 128, 128)] = block.astype(bf16)

    x, zed, core = tm // 4, lax.rem(tm // 2, 2), lax.rem(tm, 2)
    targets = {
        "sib": (x, zed, 1 - core),
        "zed": (x, 1 - zed, core),
        "right": (lax.rem(x + 1, 4), zed, core),
        "left": (lax.rem(x + 3, 4), zed, core),
        "over": (lax.rem(x + 2, 4), zed, core),
    }
    targets = {name: tx * 4 + tz * 2 + tc for name, (tx, tz, tc) in targets.items()}
    moves = {"sib": (0, 0, 8), "zed": (0, 4, 0), "right": (3, 0, 0), "left": (1, 0, 0), "over": (2, 0, 0)}
    lanes = {"all": pl.ds(0, COLS), "lo": pl.ds(0, HALF), "hi": pl.ds(HALF, HALF)}
    across = [name for name in GATHER if GATHER[name][3] != "sib"]
    numbers = {name: across.index(name) if name in across else len(across) for name in GATHER}

    def sent_view(name):
        block, chans, which, _, _ = GATHER[name]
        return full.at[pl.ds(chans[0], len(chans)), PLACE[block], :, lanes[which]]

    def arrived_view(name):
        block, chans, which, target, _ = GATHER[name]
        place, (dx, dz, dc) = PLACE[block], moves[target]
        place = (place % 4 + dx) % 4 + (place // 4 * 4 + dz) % 8 + dc
        return full.at[pl.ds(chans[0], len(chans)), place, :, lanes[which]]

    def send(name):
        pltpu.make_async_remote_copy(
            src_ref=sent_view(name), dst_ref=arrived_view(name),
            send_sem=gather_send, recv_sem=gather_recv.at[numbers[name]],
            device_id={"tm": targets[GATHER[name][3]]}, device_id_type=MESH,
        ).start()

    def arrived(name):
        ref = arrived_view(name)
        pltpu.make_async_copy(ref, ref, gather_recv.at[numbers[name]]).wait()

    here = set()
    for name in GATHER:
        if not GATHER[name][4]:
            send(name)
    for name in ORDER:
        arrived(name)
        here.add(name)
        for later in GATHER:
            if name in GATHER[later][4] and here.issuperset(GATHER[later][4]):
                send(later)
    every = count_buf.at[pl.ds(0, NT - 1)]
    pltpu.make_async_copy(every, every, count_sem.at[1]).wait()
    for name in across:
        if name not in ORDER:
            arrived(name)
    sibling = full.at[:, pl.ds(NT // 2, NT // 2)]
    pltpu.make_async_copy(sibling, sibling, gather_recv.at[len(across)]).wait()
    pltpu.make_async_copy(every, every, count_sem.at[0]).wait()
    gone = send_buf.at[pl.ds(0, NF - 1)]
    pltpu.make_async_copy(gone, gone, turn_sem.at[0]).wait()
    @pl.when(tm < NT - 1)
    def _():
        halo.wait_send()

    units = sum(len(chans) * (2 if which == "all" else 1) for _, chans, which, _, _ in GATHER.values())
    all_sent = full.at[:, pl.ds(0, units // 4)]
    pltpu.make_async_copy(all_sent, all_sent, gather_send).wait()


def correlate(full, count_buf, out_re, out_im, stage_re, stage_im, store_sem):
    f32 = jnp.float32
    bf16 = jnp.bfloat16
    tm = lax.axis_index("tm")
    inverse = 1.0 / jnp.maximum(jnp.sum(count_buf[...], axis=0), 1.0)
    mine = pl.ds(pl.multiple_of(tm * 128, 128), 128)
    odd = (lax.broadcasted_iota(jnp.int32, (256, 128), 0) & 2) > 0
    stores = []
    for kl in range(2):
        left = full[kl, :, :, mine].reshape(256, 128).astype(f32)
        swapped = jnp.where(odd, -pltpu.roll(left, 2, 0), pltpu.roll(left, 254, 0))
        both = jnp.concatenate([left.T, swapped.T], axis=0).astype(bf16)
        factor = inverse[4 * kl : 4 * kl + 1, 0:1]
        for n in range(COLS // WIDE):
            cols = pl.ds(n * WIDE, WIDE)
            right = full[kl, :, :, cols].reshape(256, WIDE)
            result = jnp.dot(both, right, preferred_element_type=f32) * factor
            stage_re[kl, :, cols] = result[:128].astype(bf16)
            stage_im[kl, :, cols] = result[128:].astype(bf16)
            for part, (stage, out) in enumerate(((stage_re, out_re), (stage_im, out_im))):
                store = pltpu.make_async_copy(stage.at[kl, :, cols], out.at[kl, :, cols], store_sem.at[kl, n, part])
                store.start()
                stores.append(store)
    for store in stores:
        store.wait()


def body(voltages, pfb_coeffs, flags, channel_order):
    hbm = pl.BlockSpec(memory_space=pltpu.HBM)
    vmem = pl.BlockSpec(memory_space=pltpu.VMEM)
    bf16 = jnp.bfloat16
    f32 = jnp.float32
    dma = pltpu.SemaphoreType.DMA
    args = (voltages, pfb_coeffs, flags, channel_order.reshape(1, -1))
    full, counts = pl.pallas_call(
        kernel,
        out_shape=(jax.ShapeDtypeStruct((2, NT, 16, COLS), bf16), jax.ShapeDtypeStruct((NT, 8, 128), f32)),
        in_specs=[hbm] * 4,
        out_specs=(vmem, vmem),
        scratch_shapes=[
            pltpu.VMEM((TAPS, FRAME), f32),
            pltpu.VMEM((FRAMES, 2 * NF), jnp.int32),
            pltpu.VMEM((1, 2 * NF), jnp.int32),
            pltpu.VMEM((FRAMES * INPUTS, FRAME), bf16),
            pltpu.VMEM((TAPS * NCHAN, FRAME), bf16),
            pltpu.VMEM((FRAMES * INPUTS, TAPS * NCHAN), f32),
            pltpu.VMEM((NF, 16, 128), f32),
            pltpu.VMEM((NF, 16, 128), bf16),
            pltpu.VMEM((NF, 16, 128), bf16),
            pltpu.VMEM((3 * INPUTS, NCHAN), f32),
            pltpu.VMEM((3 * INPUTS, NCHAN), f32),
            dma((3,)),
            dma((FRAMES,)),
            dma((2,)),
            dma((2,)),
            dma((2,)),
            dma,
            dma((EVENTS,)),
            dma((1,)),
        ],
        compiler_params=pltpu.CompilerParams(
            collective_id=0, has_side_effects=True, vmem_limit_bytes=24 * 1024 * 1024
        ),
        name="channelize_gather",
    )(*(pltpu.with_memory_space_constraint(a, pltpu.HBM) for a in args))
    out = jax.ShapeDtypeStruct((2, 128, COLS), bf16)
    return pl.pallas_call(
        correlate,
        out_shape=(out, out),
        in_specs=[vmem, vmem],
        out_specs=(hbm, hbm),
        scratch_shapes=[
            pltpu.VMEM((2, 128, COLS), bf16),
            pltpu.VMEM((2, 128, COLS), bf16),
            dma((2, COLS // WIDE, 2)),
        ],
        compiler_params=pltpu.CompilerParams(vmem_limit_bytes=24 * 1024 * 1024),
        name="correlate",
    )(full, counts)


def solution(mesh):
    return jax.shard_map(
        body,
        mesh=mesh,
        in_specs=(P("feed", "tm"), P(), P("tm", None), P()),
        out_specs=(P("feed", "tm", None), P("feed", "tm", None)),
        check_vma=False,
    )
```

```python
import functools
import math

import jax
import jax.numpy as jnp
from jax import lax
from jax.experimental import pallas as pl
from jax.experimental.pallas import tpu as pltpu
from jax.sharding import PartitionSpec as P

CHAN0 = 448
NF = 32
NT = 16
INPUTS = 64
FRAMES = 8
TAPS = 4
FRAME = 2048
COLS = 2048
HALF = COLS // 2
WIDE = 512
NCHAN = 4 * NF
MESH = pl.DeviceIdType.MESH
SINE = [(math.pi / 2) ** n / math.factorial(n) * (-1) ** (n // 2) for n in (1, 3, 5, 7, 9, 11)]

BOTH = (0, 1)
GATHER = {
    "own0z": ("own", (0,), "all", "zed", ()),
    "own1r": ("own", (1,), "all", "right", ()),
    "own1l": ("own", (1,), "all", "left", ()),
    "own1o": ("own", (1,), "all", "over", ()),
    "own1z": ("own", (1,), "all", "zed", ()),
    "own0r": ("own", (0,), "all", "right", ()),
    "own0l": ("own", (0,), "all", "left", ()),
    "owns": ("own", BOTH, "all", "sib", ()),
    "z0r": ("z", (0,), "all", "right", ("own0z",)),
    "z0l": ("z", (0,), "all", "left", ("own0z",)),
    "z0o": ("z", (0,), "all", "over", ("own0z",)),
    "l1z": ("l", (1,), "all", "zed", ("own1r",)),
    "r1z": ("r", (1,), "all", "zed", ("own1l",)),
    "o1z": ("o", (1,), "all", "zed", ("own1o",)),
    "l0r": ("l", (0,), "lo", "right", ("own0r",)),
    "r0l": ("r", (0,), "hi", "left", ("own0l",)),
    "zs": ("z", BOTH, "all", "sib", ("own0z", "own1z")),
    "ls": ("l", BOTH, "all", "sib", ("own1r", "own0r")),
    "rs": ("r", BOTH, "all", "sib", ("own1l", "own0l")),
    "lzs": ("lz", BOTH, "all", "sib", ("z0r", "l1z")),
    "rzs": ("rz", BOTH, "all", "sib", ("z0l", "r1z")),
    "os": ("o", BOTH, "all", "sib", ("own1o", "l0r", "r0l")),
    "ozs": ("oz", BOTH, "all", "sib", ("z0o", "o1z")),
}
EVENTS = len(GATHER)
PLACE = {"own": 0, "r": 1, "o": 2, "l": 3, "z": 4, "rz": 5, "oz": 6, "lz": 7}
ORDER = ("own0z", "own1r", "own1l", "own1z", "own1o", "own0r", "own0l", "z0r", "l1z", "z0l", "r1z", "l0r", "r0l", "z0o", "o1z")

FAR = sorted(
    ((dz, dy) for dz in range(4) for dy in range(8) if dz or dy),
    key=lambda step: -(2 * min(step[0], 4 - step[0]) + min(step[1], 8 - step[1])),
)


def kernel(volt, coef_hbm, flags_hbm, order_hbm, full, count_buf, coef, flags, order, frames, table, prod,
           rows, send_buf, recv_buf, next_buf, prev_buf,
           small_sem, load_sem, next_sem, turn_sem, count_sem, gather_send, gather_recv, own_sem):
    f32 = jnp.float32
    bf16 = jnp.bfloat16
    feed = lax.axis_index("feed")
    tm = lax.axis_index("tm")

    z_hi, y = feed // 8, lax.rem(feed, 8)
    after = lax.rem(tm + 1, NT)

    def feed_at(dz, dy):
        return lax.rem(z_hi + dz, 4) * 8 + lax.rem(y + dy, 8)

    barrier = pltpu.get_barrier_semaphore()

    def greet(feed_to, tm_to):
        pl.semaphore_signal(barrier, inc=1, device_id={"feed": feed_to, "tm": tm_to}, device_id_type=MESH)

    for step in FAR[:8]:
        greet(feed_at(*step), tm)
    smalls = [
        pltpu.make_async_copy(src, dst, small_sem.at[n])
        for n, (src, dst) in enumerate(((order_hbm, order), (coef_hbm, coef), (flags_hbm, flags)))
    ]
    for small in smalls:
        small.start()
    loads = []
    for f in (7, 6, 5, 4, 3, 2, 1, 0):
        load = pltpu.make_async_copy(
            volt.at[:, pl.ds(f * FRAME, FRAME)], frames.at[pl.ds(f * INPUTS, INPUTS), :], load_sem.at[f]
        )
        load.start()
        loads.append(load)
    for step in FAR[8:]:
        greet(feed_at(*step), tm)
    for step in range(1, NT):
        greet(feed, lax.rem(tm + step, NT))

    for small in smalls:
        small.wait()

    c_row = lax.broadcasted_iota(jnp.int32, (NCHAN, 2 * NF), 0)
    k_col = lax.broadcasted_iota(jnp.int32, (NCHAN, 2 * NF), 1)
    pick = k_col == 2 * (c_row & (NF - 1)) + (c_row >> 6)
    order_f = order[...].astype(f32)
    place = jnp.sum(jnp.where(pick, order_f, 0.0), axis=1, keepdims=True)
    chan_of = place.astype(jnp.int32)
    freq = jnp.broadcast_to(chan_of + CHAN0, (NCHAN, 128))
    lane = lax.broadcasted_iota(jnp.int32, (NCHAN, 128), 1)
    part = (lax.broadcasted_iota(jnp.int32, (NCHAN, 128), 0) >> 5) & 1
    scale = (TAPS * FRAME / 2.0) ** (-0.5)

    def trig(phase):
        dist = jnp.abs((phase & (FRAME - 1)) - FRAME // 2).astype(f32)
        z = dist * (4.0 / FRAME) - 1.0
        z2 = z * z
        value = jnp.full_like(z, SINE[-1])
        for power in SINE[-2::-1]:
            value = value * z2 + power
        return value * z

    quarter = FRAME // 4
    first = trig(freq * lane + part * quarter)
    turn_cos = trig(freq * 128)
    turn_sin = trig(freq * 128 - quarter)
    signed = jnp.where(part == 0, turn_sin, -turn_sin)

    def table_block(a, value):
        cols = pl.ds(pl.multiple_of(a * 128, 128), 128)
        for t in range(TAPS):
            table[pl.ds(t * NCHAN, NCHAN), cols] = (value * (coef[pl.ds(t, 1), cols] * scale)).astype(bf16)
        swapped = jnp.concatenate([value[n * NF : (n + 1) * NF] for n in (1, 0, 3, 2)], axis=0)
        return value * turn_cos + swapped * signed

    lax.fori_loop(0, FRAME // 128, table_block, first)

    hot = (lax.broadcasted_iota(jnp.int32, (NCHAN, 2 * NF), 1) == chan_of).astype(bf16)
    nt = (((1,), (1,)), ((), ()))
    good = lax.dot_general(flags[...].astype(f32).astype(bf16), hot, nt, preferred_element_type=f32)
    local = jnp.sum(good, axis=0, keepdims=True)
    lane1 = lax.broadcasted_iota(jnp.int32, (1, NCHAN), 1)
    counts = [
        jnp.sum(jnp.where(lane1 == feed + kl * 2 * NF, local, 0.0), axis=1, keepdims=True) for kl in range(2)
    ]
    sub8 = lax.broadcasted_iota(jnp.int32, (8, 128), 0)
    count_buf[tm] = jnp.where(sub8 < 4, counts[0], counts[1])

    for load in loads[:4]:
        load.wait()
    prod[pl.ds(256, 256), :] = lax.dot_general(
        frames[pl.ds(256, 256), :], table[...], nt, preferred_element_type=f32
    )

    def term(f, t):
        return prod[pl.ds(f * INPUTS, INPUTS), pl.ds(t * NCHAN, NCHAN)]

    def partial(s):
        terms = [term(s - 3 + t, t) for t in range(TAPS) if 0 <= s - 3 + t < FRAMES]
        total = terms[0]
        for other in terms[1:]:
            total = total + other
        return total

    for s in range(3):
        next_buf[pl.ds(s * INPUTS, INPUTS), :] = partial(FRAMES + s).astype(next_buf.dtype)
    pl.semaphore_wait(barrier, NF - 1 + NT - 1)
    halo = pltpu.make_async_remote_copy(
        src_ref=next_buf, dst_ref=prev_buf, send_sem=next_sem.at[0], recv_sem=next_sem.at[1],
        device_id={"tm": after}, device_id_type=MESH,
    )
    @pl.when(tm < NT - 1)
    def _():
        halo.start()

    for load in loads[4:]:
        load.wait()
    prod[pl.ds(0, 256), :] = lax.dot_general(
        frames[pl.ds(0, 256), :], table[...], nt, preferred_element_type=f32
    )

    def total(s):
        value = partial(s)
        if s < 3:
            value = value + jnp.where(tm > 0, prev_buf[pl.ds(s * INPUTS, INPUTS), :].astype(f32), 0.0)
        return value

    def turn(j):
        turned = jnp.concatenate([total(2 * j), total(2 * j + 1)], axis=0).T
        for q in range(4):
            rows[:, (q // 2) * 8 + (j // 2) * 4 + (q % 2) * 2 + j % 2, :] = turned[q * NF : (q + 1) * NF, :]

    turn(3)
    turn(2)
    @pl.when(tm > 0)
    def _():
        halo.wait_recv()

    turn(1)
    turn(0)
    send_buf[...] = rows[...].astype(bf16)

    for step in FAR:
        peer = feed_at(*step)
        pltpu.make_async_remote_copy(
            src_ref=send_buf.at[peer], dst_ref=recv_buf.at[feed],
            send_sem=turn_sem.at[0], recv_sem=turn_sem.at[1],
            device_id={"feed": peer, "tm": tm}, device_id_type=MESH,
        ).start()
    own = pltpu.make_async_copy(send_buf.at[feed], recv_buf.at[feed], own_sem.at[0])
    own.start()

    def send_count(step, carry):
        pltpu.make_async_remote_copy(
            src_ref=count_buf.at[tm], dst_ref=count_buf.at[tm],
            send_sem=count_sem.at[0], recv_sem=count_sem.at[1],
            device_id={"tm": lax.rem(tm + step, NT)}, device_id_type=MESH,
        ).start()
        return carry

    lax.fori_loop(1, NT, send_count, 0)

    row = lax.broadcasted_iota(jnp.int32, (32, FRAMES), 0)
    spec = (row & 1) * 2 + ((row >> 2) & 1) * 4 + (row >> 4)
    match = (spec == lax.broadcasted_iota(jnp.int32, (32, FRAMES), 1)).astype(bf16)
    every_flag = jnp.dot(match, good.astype(bf16), preferred_element_type=f32)
    row = lax.broadcasted_iota(jnp.int32, (32, NCHAN), 0)
    mine = lax.broadcasted_iota(jnp.int32, (32, NCHAN), 1) == feed + ((row >> 3) & 1) * 2 * NF
    clean = jnp.sum(jnp.where(mine, every_flag, 0.0), axis=1, keepdims=True)

    own.wait()
    others = recv_buf.at[pl.ds(0, NF - 1)]
    pltpu.make_async_copy(others, others, turn_sem.at[1]).wait()

    low = lax.broadcasted_iota(jnp.int32, (16, 128), 1) < INPUTS
    for g in range(NF // 2):
        one = recv_buf[2 * g].astype(f32)
        two = recv_buf[2 * g + 1].astype(f32)
        first = jnp.where(low, one, pltpu.roll(two, INPUTS, 1)) * clean[:16]
        second = jnp.where(low, pltpu.roll(one, INPUTS, 1), two) * clean[16:]
        for kl in range(2):
            block = jnp.concatenate([first[kl * 8 : kl * 8 + 8], second[kl * 8 : kl * 8 + 8]], axis=0)
            full[kl, 0, :, pl.ds(g * 128, 128)] = block.astype(bf16)

    x, zed, core = tm // 4, lax.rem(tm // 2, 2), lax.rem(tm, 2)
    targets = {
        "sib": (x, zed, 1 - core),
        "zed": (x, 1 - zed, core),
        "right": (lax.rem(x + 1, 4), zed, core),
        "left": (lax.rem(x + 3, 4), zed, core),
        "over": (lax.rem(x + 2, 4), zed, core),
    }
    targets = {name: tx * 4 + tz * 2 + tc for name, (tx, tz, tc) in targets.items()}
    moves = {"sib": (0, 0, 8), "zed": (0, 4, 0), "right": (3, 0, 0), "left": (1, 0, 0), "over": (2, 0, 0)}
    lanes = {"all": pl.ds(0, COLS), "lo": pl.ds(0, HALF), "hi": pl.ds(HALF, HALF)}
    across = [name for name in GATHER if GATHER[name][3] != "sib"]
    numbers = {name: across.index(name) if name in across else len(across) for name in GATHER}

    def sent_view(name):
        block, chans, which, _, _ = GATHER[name]
        return full.at[pl.ds(chans[0], len(chans)), PLACE[block], :, lanes[which]]

    def arrived_view(name):
        block, chans, which, target, _ = GATHER[name]
        place, (dx, dz, dc) = PLACE[block], moves[target]
        place = (place % 4 + dx) % 4 + (place // 4 * 4 + dz) % 8 + dc
        return full.at[pl.ds(chans[0], len(chans)), place, :, lanes[which]]

    def send(name):
        pltpu.make_async_remote_copy(
            src_ref=sent_view(name), dst_ref=arrived_view(name),
            send_sem=gather_send, recv_sem=gather_recv.at[numbers[name]],
            device_id={"tm": targets[GATHER[name][3]]}, device_id_type=MESH,
        ).start()

    def arrived(name):
        ref = arrived_view(name)
        pltpu.make_async_copy(ref, ref, gather_recv.at[numbers[name]]).wait()

    here = set()
    for name in GATHER:
        if not GATHER[name][4]:
            send(name)
    for name in ORDER:
        arrived(name)
        here.add(name)
        for later in GATHER:
            if name in GATHER[later][4] and here.issuperset(GATHER[later][4]):
                send(later)
    every = count_buf.at[pl.ds(0, NT - 1)]
    pltpu.make_async_copy(every, every, count_sem.at[1]).wait()
    for name in across:
        if name not in ORDER:
            arrived(name)
    sibling = full.at[:, pl.ds(NT // 2, NT // 2)]
    pltpu.make_async_copy(sibling, sibling, gather_recv.at[len(across)]).wait()
    pltpu.make_async_copy(every, every, count_sem.at[0]).wait()
    gone = send_buf.at[pl.ds(0, NF - 1)]
    pltpu.make_async_copy(gone, gone, turn_sem.at[0]).wait()
    @pl.when(tm < NT - 1)
    def _():
        halo.wait_send()

    units = sum(len(chans) * (2 if which == "all" else 1) for _, chans, which, _, _ in GATHER.values())
    all_sent = full.at[:, pl.ds(0, units // 4)]
    pltpu.make_async_copy(all_sent, all_sent, gather_send).wait()


def correlate(full, count_buf, out_re, out_im, stage_re, stage_im, store_sem):
    f32 = jnp.float32
    bf16 = jnp.bfloat16
    tm = lax.axis_index("tm")
    inverse = 1.0 / jnp.maximum(jnp.sum(count_buf[...], axis=0), 1.0)
    mine = pl.ds(pl.multiple_of(tm * 128, 128), 128)
    odd = (lax.broadcasted_iota(jnp.int32, (256, 128), 0) & 2) > 0
    stores = []
    for kl in range(2):
        left = full[kl, :, :, mine].reshape(256, 128).astype(f32)
        swapped = jnp.where(odd, -pltpu.roll(left, 2, 0), pltpu.roll(left, 254, 0))
        both = jnp.concatenate([left.T, swapped.T], axis=0).astype(bf16)
        factor = inverse[4 * kl : 4 * kl + 1, 0:1]
        for n in range(COLS // WIDE):
            cols = pl.ds(n * WIDE, WIDE)
            right = full[kl, :, :, cols].reshape(256, WIDE)
            result = jnp.dot(both, right, preferred_element_type=f32) * factor
            stage_re[kl, :, cols] = result[:128].astype(bf16)
            stage_im[kl, :, cols] = result[128:].astype(bf16)
            for part, (stage, out) in enumerate(((stage_re, out_re), (stage_im, out_im))):
                store = pltpu.make_async_copy(stage.at[kl, :, cols], out.at[kl, :, cols], store_sem.at[kl, n, part])
                store.start()
                stores.append(store)
    for store in stores:
        store.wait()


def body(voltages, pfb_coeffs, flags, channel_order):
    hbm = pl.BlockSpec(memory_space=pltpu.HBM)
    vmem = pl.BlockSpec(memory_space=pltpu.VMEM)
    bf16 = jnp.bfloat16
    f32 = jnp.float32
    dma = pltpu.SemaphoreType.DMA
    args = (voltages, pfb_coeffs, flags, channel_order.reshape(1, -1))
    full, counts = pl.pallas_call(
        kernel,
        out_shape=(jax.ShapeDtypeStruct((2, NT, 16, COLS), bf16), jax.ShapeDtypeStruct((NT, 8, 128), f32)),
        in_specs=[hbm] * 4,
        out_specs=(vmem, vmem),
        scratch_shapes=[
            pltpu.VMEM((TAPS, FRAME), f32),
            pltpu.VMEM((FRAMES, 2 * NF), jnp.int32),
            pltpu.VMEM((1, 2 * NF), jnp.int32),
            pltpu.VMEM((FRAMES * INPUTS, FRAME), bf16),
            pltpu.VMEM((TAPS * NCHAN, FRAME), bf16),
            pltpu.VMEM((FRAMES * INPUTS, TAPS * NCHAN), f32),
            pltpu.VMEM((NF, 16, 128), f32),
            pltpu.VMEM((NF, 16, 128), bf16),
            pltpu.VMEM((NF, 16, 128), bf16),
            pltpu.VMEM((3 * INPUTS, NCHAN), bf16),
            pltpu.VMEM((3 * INPUTS, NCHAN), bf16),
            dma((3,)),
            dma((FRAMES,)),
            dma((2,)),
            dma((2,)),
            dma((2,)),
            dma,
            dma((EVENTS,)),
            dma((1,)),
        ],
        compiler_params=pltpu.CompilerParams(
            collective_id=0, has_side_effects=True, vmem_limit_bytes=24 * 1024 * 1024
        ),
        name="channelize_gather",
    )(*(pltpu.with_memory_space_constraint(a, pltpu.HBM) for a in args))
    out = jax.ShapeDtypeStruct((2, 128, COLS), bf16)
    return pl.pallas_call(
        correlate,
        out_shape=(out, out),
        in_specs=[vmem, vmem],
        out_specs=(hbm, hbm),
        scratch_shapes=[
            pltpu.VMEM((2, 128, COLS), bf16),
            pltpu.VMEM((2, 128, COLS), bf16),
            dma((2, COLS // WIDE, 2)),
        ],
        compiler_params=pltpu.CompilerParams(vmem_limit_bytes=24 * 1024 * 1024),
        name="correlate",
    )(full, counts)


def solution(mesh):
    return jax.shard_map(
        body,
        mesh=mesh,
        in_specs=(P("feed", "tm"), P(), P("tm", None), P()),
        out_specs=(P("feed", "tm", None), P("feed", "tm", None)),
        check_vma=False,
    )
```

```python
import functools
import math

import jax
import jax.numpy as jnp
from jax import lax
from jax.experimental import pallas as pl
from jax.experimental.pallas import tpu as pltpu
from jax.sharding import PartitionSpec as P

CHAN0 = 448
NF = 32
NT = 16
INPUTS = 64
FRAMES = 8
TAPS = 4
FRAME = 2048
COLS = 2048
HALF = COLS // 2
WIDE = 512
NCHAN = 4 * NF
MESH = pl.DeviceIdType.MESH
SINE = [(math.pi / 2) ** n / math.factorial(n) * (-1) ** (n // 2) for n in (1, 3, 5, 7, 9, 11)]

BOTH = (0, 1)
GATHER = {
    "own0z": ("own", (0,), "all", "zed", ()),
    "own1r": ("own", (1,), "all", "right", ()),
    "own1l": ("own", (1,), "all", "left", ()),
    "own1o": ("own", (1,), "all", "over", ()),
    "own1z": ("own", (1,), "all", "zed", ()),
    "own0r": ("own", (0,), "all", "right", ()),
    "own0l": ("own", (0,), "all", "left", ()),
    "owns": ("own", BOTH, "all", "sib", ()),
    "z0r": ("z", (0,), "all", "right", ("own0z",)),
    "z0l": ("z", (0,), "all", "left", ("own0z",)),
    "z0o": ("z", (0,), "all", "over", ("own0z",)),
    "l1z": ("l", (1,), "all", "zed", ("own1r",)),
    "r1z": ("r", (1,), "all", "zed", ("own1l",)),
    "o1z": ("o", (1,), "all", "zed", ("own1o",)),
    "l0r": ("l", (0,), "lo", "right", ("own0r",)),
    "r0l": ("r", (0,), "hi", "left", ("own0l",)),
    "zs": ("z", BOTH, "all", "sib", ("own0z", "own1z")),
    "ls": ("l", BOTH, "all", "sib", ("own1r", "own0r")),
    "rs": ("r", BOTH, "all", "sib", ("own1l", "own0l")),
    "lzs": ("lz", BOTH, "all", "sib", ("z0r", "l1z")),
    "rzs": ("rz", BOTH, "all", "sib", ("z0l", "r1z")),
    "os": ("o", BOTH, "all", "sib", ("own1o", "l0r", "r0l")),
    "ozs": ("oz", BOTH, "all", "sib", ("z0o", "o1z")),
}
EVENTS = len(GATHER)
PLACE = {"own": 0, "r": 1, "o": 2, "l": 3, "z": 4, "rz": 5, "oz": 6, "lz": 7}
ORDER = ("own0z", "own1r", "own1l", "own1z", "own1o", "own0r", "own0l", "z0r", "l1z", "z0l", "r1z", "l0r", "r0l", "z0o", "o1z")

FAR = sorted(
    ((dz, dy) for dz in range(4) for dy in range(8) if dz or dy),
    key=lambda step: -(2 * min(step[0], 4 - step[0]) + min(step[1], 8 - step[1])),
)


def kernel(volt, coef_hbm, flags_hbm, order_hbm, full, count_buf, coef, flags, order, frames, table, prod,
           rows, send_buf, recv_buf, next_buf, prev_buf,
           small_sem, load_sem, next_sem, turn_sem, count_sem, gather_send, gather_recv, own_sem):
    f32 = jnp.float32
    bf16 = jnp.bfloat16
    feed = lax.axis_index("feed")
    tm = lax.axis_index("tm")

    z_hi, y = feed // 8, lax.rem(feed, 8)
    after = lax.rem(tm + 1, NT)

    def feed_at(dz, dy):
        return lax.rem(z_hi + dz, 4) * 8 + lax.rem(y + dy, 8)

    barrier = pltpu.get_barrier_semaphore()

    def greet(feed_to, tm_to):
        pl.semaphore_signal(barrier, inc=1, device_id={"feed": feed_to, "tm": tm_to}, device_id_type=MESH)

    for step in FAR[:8]:
        greet(feed_at(*step), tm)
    smalls = [
        pltpu.make_async_copy(src, dst, small_sem.at[n])
        for n, (src, dst) in enumerate(((order_hbm, order), (coef_hbm, coef), (flags_hbm, flags)))
    ]
    for small in smalls:
        small.start()
    loads = []
    for f in (7, 6, 5, 4, 3, 2, 1, 0):
        load = pltpu.make_async_copy(
            volt.at[:, pl.ds(f * FRAME, FRAME)], frames.at[pl.ds(f * INPUTS, INPUTS), :], load_sem.at[f]
        )
        load.start()
        loads.append(load)
    for step in FAR[8:]:
        greet(feed_at(*step), tm)
    for step in range(1, NT):
        greet(feed, lax.rem(tm + step, NT))

    for small in smalls:
        small.wait()

    c_row = lax.broadcasted_iota(jnp.int32, (NCHAN, 2 * NF), 0)
    k_col = lax.broadcasted_iota(jnp.int32, (NCHAN, 2 * NF), 1)
    pick = k_col == 2 * (c_row & (NF - 1)) + (c_row >> 6)
    order_f = order[...].astype(f32)
    place = jnp.sum(jnp.where(pick, order_f, 0.0), axis=1, keepdims=True)
    chan_of = place.astype(jnp.int32)
    freq = jnp.broadcast_to(chan_of + CHAN0, (NCHAN, 128))
    lane = lax.broadcasted_iota(jnp.int32, (NCHAN, 128), 1)
    part = (lax.broadcasted_iota(jnp.int32, (NCHAN, 128), 0) >> 5) & 1
    scale = (TAPS * FRAME / 2.0) ** (-0.5)

    def trig(phase):
        dist = jnp.abs((phase & (FRAME - 1)) - FRAME // 2).astype(f32)
        z = dist * (4.0 / FRAME) - 1.0
        z2 = z * z
        value = jnp.full_like(z, SINE[-1])
        for power in SINE[-2::-1]:
            value = value * z2 + power
        return value * z

    quarter = FRAME // 4
    first = trig(freq * lane + part * quarter)
    turn_cos = trig(freq * 128)
    turn_sin = trig(freq * 128 - quarter)
    signed = jnp.where(part == 0, turn_sin, -turn_sin)

    def table_block(a, value):
        cols = pl.ds(pl.multiple_of(a * 128, 128), 128)
        for t in range(TAPS):
            table[pl.ds(t * NCHAN, NCHAN), cols] = (value * (coef[pl.ds(t, 1), cols] * scale)).astype(bf16)
        swapped = jnp.concatenate([value[n * NF : (n + 1) * NF] for n in (1, 0, 3, 2)], axis=0)
        return value * turn_cos + swapped * signed

    lax.fori_loop(0, FRAME // 128, table_block, first)

    hot = (lax.broadcasted_iota(jnp.int32, (NCHAN, 2 * NF), 1) == chan_of).astype(bf16)
    nt = (((1,), (1,)), ((), ()))
    good = lax.dot_general(flags[...].astype(f32).astype(bf16), hot, nt, preferred_element_type=f32)
    local = jnp.sum(good, axis=0, keepdims=True)
    lane1 = lax.broadcasted_iota(jnp.int32, (1, NCHAN), 1)
    counts = [
        jnp.sum(jnp.where(lane1 == feed + kl * 2 * NF, local, 0.0), axis=1, keepdims=True) for kl in range(2)
    ]
    sub8 = lax.broadcasted_iota(jnp.int32, (8, 128), 0)
    count_buf[tm] = jnp.where(sub8 < 4, counts[0], counts[1])

    for load in loads[:3]:
        load.wait()
    prod[pl.ds(320, 192), pl.ds(0, 384)] = lax.dot_general(
        frames[pl.ds(320, 192), :], table[pl.ds(0, 384), :], nt, preferred_element_type=f32
    )

    def term(f, t):
        return prod[pl.ds(f * INPUTS, INPUTS), pl.ds(t * NCHAN, NCHAN)]

    def partial(s):
        terms = [term(s - 3 + t, t) for t in range(TAPS) if 0 <= s - 3 + t < FRAMES]
        total = terms[0]
        for other in terms[1:]:
            total = total + other
        return total

    for s in range(3):
        next_buf[pl.ds(s * INPUTS, INPUTS), :] = partial(FRAMES + s).astype(next_buf.dtype)
    pl.semaphore_wait(barrier, NF - 1 + NT - 1)
    halo = pltpu.make_async_remote_copy(
        src_ref=next_buf, dst_ref=prev_buf, send_sem=next_sem.at[0], recv_sem=next_sem.at[1],
        device_id={"tm": after}, device_id_type=MESH,
    )
    @pl.when(tm < NT - 1)
    def _():
        halo.start()

    for load in loads[3:]:
        load.wait()
    prod[pl.ds(0, 320), :] = lax.dot_general(
        frames[pl.ds(0, 320), :], table[...], nt, preferred_element_type=f32
    )
    prod[pl.ds(320, 192), pl.ds(384, 128)] = lax.dot_general(
        frames[pl.ds(320, 192), :], table[pl.ds(384, 128), :], nt, preferred_element_type=f32
    )

    def total(s):
        value = partial(s)
        if s < 3:
            value = value + jnp.where(tm > 0, prev_buf[pl.ds(s * INPUTS, INPUTS), :].astype(f32), 0.0)
        return value

    def turn(j):
        turned = jnp.concatenate([total(2 * j), total(2 * j + 1)], axis=0).T
        for q in range(4):
            rows[:, (q // 2) * 8 + (j // 2) * 4 + (q % 2) * 2 + j % 2, :] = turned[q * NF : (q + 1) * NF, :]

    turn(3)
    turn(2)
    @pl.when(tm > 0)
    def _():
        halo.wait_recv()

    turn(1)
    turn(0)
    send_buf[...] = rows[...].astype(bf16)

    for step in FAR:
        peer = feed_at(*step)
        pltpu.make_async_remote_copy(
            src_ref=send_buf.at[peer], dst_ref=recv_buf.at[feed],
            send_sem=turn_sem.at[0], recv_sem=turn_sem.at[1],
            device_id={"feed": peer, "tm": tm}, device_id_type=MESH,
        ).start()
    own = pltpu.make_async_copy(send_buf.at[feed], recv_buf.at[feed], own_sem.at[0])
    own.start()

    def send_count(step, carry):
        pltpu.make_async_remote_copy(
            src_ref=count_buf.at[tm], dst_ref=count_buf.at[tm],
            send_sem=count_sem.at[0], recv_sem=count_sem.at[1],
            device_id={"tm": lax.rem(tm + step, NT)}, device_id_type=MESH,
        ).start()
        return carry

    lax.fori_loop(1, NT, send_count, 0)

    row = lax.broadcasted_iota(jnp.int32, (32, FRAMES), 0)
    spec = (row & 1) * 2 + ((row >> 2) & 1) * 4 + (row >> 4)
    match = (spec == lax.broadcasted_iota(jnp.int32, (32, FRAMES), 1)).astype(bf16)
    every_flag = jnp.dot(match, good.astype(bf16), preferred_element_type=f32)
    row = lax.broadcasted_iota(jnp.int32, (32, NCHAN), 0)
    mine = lax.broadcasted_iota(jnp.int32, (32, NCHAN), 1) == feed + ((row >> 3) & 1) * 2 * NF
    clean = jnp.sum(jnp.where(mine, every_flag, 0.0), axis=1, keepdims=True)

    own.wait()
    others = recv_buf.at[pl.ds(0, NF - 1)]
    pltpu.make_async_copy(others, others, turn_sem.at[1]).wait()

    low = lax.broadcasted_iota(jnp.int32, (16, 128), 1) < INPUTS
    for g in range(NF // 2):
        one = recv_buf[2 * g].astype(f32)
        two = recv_buf[2 * g + 1].astype(f32)
        first = jnp.where(low, one, pltpu.roll(two, INPUTS, 1)) * clean[:16]
        second = jnp.where(low, pltpu.roll(one, INPUTS, 1), two) * clean[16:]
        for kl in range(2):
            block = jnp.concatenate([first[kl * 8 : kl * 8 + 8], second[kl * 8 : kl * 8 + 8]], axis=0)
            full[kl, 0, :, pl.ds(g * 128, 128)] = block.astype(bf16)

    x, zed, core = tm // 4, lax.rem(tm // 2, 2), lax.rem(tm, 2)
    targets = {
        "sib": (x, zed, 1 - core),
        "zed": (x, 1 - zed, core),
        "right": (lax.rem(x + 1, 4), zed, core),
        "left": (lax.rem(x + 3, 4), zed, core),
        "over": (lax.rem(x + 2, 4), zed, core),
    }
    targets = {name: tx * 4 + tz * 2 + tc for name, (tx, tz, tc) in targets.items()}
    moves = {"sib": (0, 0, 8), "zed": (0, 4, 0), "right": (3, 0, 0), "left": (1, 0, 0), "over": (2, 0, 0)}
    lanes = {"all": pl.ds(0, COLS), "lo": pl.ds(0, HALF), "hi": pl.ds(HALF, HALF)}
    across = [name for name in GATHER if GATHER[name][3] != "sib"]
    numbers = {name: across.index(name) if name in across else len(across) for name in GATHER}

    def sent_view(name):
        block, chans, which, _, _ = GATHER[name]
        return full.at[pl.ds(chans[0], len(chans)), PLACE[block], :, lanes[which]]

    def arrived_view(name):
        block, chans, which, target, _ = GATHER[name]
        place, (dx, dz, dc) = PLACE[block], moves[target]
        place = (place % 4 + dx) % 4 + (place // 4 * 4 + dz) % 8 + dc
        return full.at[pl.ds(chans[0], len(chans)), place, :, lanes[which]]

    def send(name):
        pltpu.make_async_remote_copy(
            src_ref=sent_view(name), dst_ref=arrived_view(name),
            send_sem=gather_send, recv_sem=gather_recv.at[numbers[name]],
            device_id={"tm": targets[GATHER[name][3]]}, device_id_type=MESH,
        ).start()

    def arrived(name):
        ref = arrived_view(name)
        pltpu.make_async_copy(ref, ref, gather_recv.at[numbers[name]]).wait()

    here = set()
    for name in GATHER:
        if not GATHER[name][4]:
            send(name)
    for name in ORDER:
        arrived(name)
        here.add(name)
        for later in GATHER:
            if name in GATHER[later][4] and here.issuperset(GATHER[later][4]):
                send(later)
    every = count_buf.at[pl.ds(0, NT - 1)]
    pltpu.make_async_copy(every, every, count_sem.at[1]).wait()
    for name in across:
        if name not in ORDER:
            arrived(name)
    sibling = full.at[:, pl.ds(NT // 2, NT // 2)]
    pltpu.make_async_copy(sibling, sibling, gather_recv.at[len(across)]).wait()
    pltpu.make_async_copy(every, every, count_sem.at[0]).wait()
    gone = send_buf.at[pl.ds(0, NF - 1)]
    pltpu.make_async_copy(gone, gone, turn_sem.at[0]).wait()
    @pl.when(tm < NT - 1)
    def _():
        halo.wait_send()

    units = sum(len(chans) * (2 if which == "all" else 1) for _, chans, which, _, _ in GATHER.values())
    all_sent = full.at[:, pl.ds(0, units // 4)]
    pltpu.make_async_copy(all_sent, all_sent, gather_send).wait()


def correlate(full, count_buf, out_re, out_im, stage_re, stage_im, store_sem):
    f32 = jnp.float32
    bf16 = jnp.bfloat16
    tm = lax.axis_index("tm")
    inverse = 1.0 / jnp.maximum(jnp.sum(count_buf[...], axis=0), 1.0)
    mine = pl.ds(pl.multiple_of(tm * 128, 128), 128)
    odd = (lax.broadcasted_iota(jnp.int32, (256, 128), 0) & 2) > 0
    stores = []
    for kl in range(2):
        left = full[kl, :, :, mine].reshape(256, 128).astype(f32)
        swapped = jnp.where(odd, -pltpu.roll(left, 2, 0), pltpu.roll(left, 254, 0))
        both = jnp.concatenate([left.T, swapped.T], axis=0).astype(bf16)
        factor = inverse[4 * kl : 4 * kl + 1, 0:1]
        for n in range(COLS // WIDE):
            cols = pl.ds(n * WIDE, WIDE)
            right = full[kl, :, :, cols].reshape(256, WIDE)
            result = jnp.dot(both, right, preferred_element_type=f32) * factor
            stage_re[kl, :, cols] = result[:128].astype(bf16)
            stage_im[kl, :, cols] = result[128:].astype(bf16)
            for part, (stage, out) in enumerate(((stage_re, out_re), (stage_im, out_im))):
                store = pltpu.make_async_copy(stage.at[kl, :, cols], out.at[kl, :, cols], store_sem.at[kl, n, part])
                store.start()
                stores.append(store)
    for store in stores:
        store.wait()


def body(voltages, pfb_coeffs, flags, channel_order):
    hbm = pl.BlockSpec(memory_space=pltpu.HBM)
    vmem = pl.BlockSpec(memory_space=pltpu.VMEM)
    bf16 = jnp.bfloat16
    f32 = jnp.float32
    dma = pltpu.SemaphoreType.DMA
    args = (voltages, pfb_coeffs, flags, channel_order.reshape(1, -1))
    full, counts = pl.pallas_call(
        kernel,
        out_shape=(jax.ShapeDtypeStruct((2, NT, 16, COLS), bf16), jax.ShapeDtypeStruct((NT, 8, 128), f32)),
        in_specs=[hbm] * 4,
        out_specs=(vmem, vmem),
        scratch_shapes=[
            pltpu.VMEM((TAPS, FRAME), f32),
            pltpu.VMEM((FRAMES, 2 * NF), jnp.int32),
            pltpu.VMEM((1, 2 * NF), jnp.int32),
            pltpu.VMEM((FRAMES * INPUTS, FRAME), bf16),
            pltpu.VMEM((TAPS * NCHAN, FRAME), bf16),
            pltpu.VMEM((FRAMES * INPUTS, TAPS * NCHAN), f32),
            pltpu.VMEM((NF, 16, 128), f32),
            pltpu.VMEM((NF, 16, 128), bf16),
            pltpu.VMEM((NF, 16, 128), bf16),
            pltpu.VMEM((3 * INPUTS, NCHAN), bf16),
            pltpu.VMEM((3 * INPUTS, NCHAN), bf16),
            dma((3,)),
            dma((FRAMES,)),
            dma((2,)),
            dma((2,)),
            dma((2,)),
            dma,
            dma((EVENTS,)),
            dma((1,)),
        ],
        compiler_params=pltpu.CompilerParams(
            collective_id=0, has_side_effects=True, vmem_limit_bytes=24 * 1024 * 1024
        ),
        name="channelize_gather",
    )(*(pltpu.with_memory_space_constraint(a, pltpu.HBM) for a in args))
    out = jax.ShapeDtypeStruct((2, 128, COLS), bf16)
    return pl.pallas_call(
        correlate,
        out_shape=(out, out),
        in_specs=[vmem, vmem],
        out_specs=(hbm, hbm),
        scratch_shapes=[
            pltpu.VMEM((2, 128, COLS), bf16),
            pltpu.VMEM((2, 128, COLS), bf16),
            dma((2, COLS // WIDE, 2)),
        ],
        compiler_params=pltpu.CompilerParams(vmem_limit_bytes=24 * 1024 * 1024),
        name="correlate",
    )(full, counts)


def solution(mesh):
    return jax.shard_map(
        body,
        mesh=mesh,
        in_specs=(P("feed", "tm"), P(), P("tm", None), P()),
        out_specs=(P("feed", "tm", None), P("feed", "tm", None)),
        check_vma=False,
    )
```
